128 devices in a mesh: dyn: 32 (over y, x, core), rad: 4 (over z).
Axes of the slice: x: 4, y: 4, z: 4, core: 2. Of those that a mesh axis runs over, the one named last changes fastest.
Arguments:
- thermal_profile: float32 [137, 262144], P(None, ('dyn', 'rad')), may hold values from 0.6 to 1.4
- gas_loadings: float32 [4, 137, 262144], P(None, None, ('dyn', 'rad')), may hold values from 0.05 to 2
- profile_footprint: float32 [262144], P(('dyn', 'rad')), may hold values from 1 to 4
- profile_segment: int32 [262144], P(('dyn', 'rad')), may hold values from 0 to 511
- segment_holder_chip: int32 [65536, 1], P(('dyn', 'rad')), may hold values from 0 to 127; in each aligned block of 512 rows (0 to 511, 512 to 1023, ...) at most 8 rows name the same one
- segment_box_local: int32 [65536], P(('dyn', 'rad')), may hold values from 0 to 255
- opacity_table: float32 [32, 4], replicated, may hold values from 0.002 to 0.5
- blackbody_fraction: float32 [32], replicated, may hold values from 0.02 to 0.1
Outputs:
- heating: float32 [137, 262144], P(None, ('dyn', 'rad'))
The draws below stay inside these ranges and needn't reach their ends.
Inputs may be any that keep to these rules, and one draw needn't show every extreme that they name: `segment_holder_chip`: among the 512 pieces of one device, at most 8 name the same owner device.
All inputs are finite; a program needn't handle non-finite values.
Results may differ from the reference program's by a relative error of at most 0.0003.
Values sent between devices are 32-bit elements; how exact they have to be, the bound alone decides.
No kernel may reach another device: no remote copies, remote signals or barrier semaphores. Data moves between devices by JAX's collectives and lax.ppermute only.
A program may use at most 128 MiB of HBM per device.

```python
import math
import jax
import jax.numpy as jnp
import numpy as np
from jax import lax

HEIGHT_LAYERS = 137
G = 32
NABS = 4
F_DEV = 2048
P_DEV = 512
C_DEV = 256
CAP = 8
TOTAL_PROFILES = 262144
NPIECE = 65536
NCOARSE = 32768
DEVICES = 128


def place_ends(result, rng, low, largest):
    extent = result.shape
    place = [jax.random.randint(jax.random.fold_in(rng, axis), (), 0, extent[axis]) for axis in range(len(extent))]
    result = result.at[tuple(place)].set(low)
    longest = extent.index(max(extent))
    place[longest] = (place[longest] + 1) % extent[longest]
    return result.at[tuple(place)].set(largest)


def levels(rng, shape, split, least, high):
    factor_of, own = 1.0, jax.random.fold_in(rng, 6)
    for dim, blocks in split:
        steps = jnp.exp(jax.random.uniform(jax.random.fold_in(own, dim), (blocks,), jnp.float32, least / len(split), high / len(split)))
        factor_of = factor_of * jnp.repeat(steps, shape[dim] // blocks).reshape([-1 if axis == dim else 1 for axis in range(len(shape))])
    return factor_of


def deal_out(own_key, own, number, rows, count, top, most, skew):
    sequence = jax.random.permutation(own_key, count)
    crowded, usual = shares(count, rows * top, most, skew, True), shares(count, rows * top, most, skew, False)
    places = jnp.arange(count)

    def named(lengths, turn):
        used = int((lengths > 0).sum())
        fixed = max(1, used // 4)
        moved = fixed + (places - fixed + turn * (used - fixed)) % max(1, count - fixed)
        return jnp.zeros((count,), jnp.int32).at[sequence[jnp.where(places < fixed, places, moved)]].set(jnp.asarray(lengths, jnp.int32))

    lengths = jnp.where(number % 4 == 0, named(crowded, number // 4), named(usual, number - number // 4 - 1))
    mixed = jax.random.permutation(jax.random.fold_in(own, 3), count)
    giver, receiver = mixed[0:count // 2 * 2:2], mixed[1:count // 2 * 2:2]
    slack = jnp.minimum(lengths[giver] - 1, most - lengths[receiver]) // 2
    slack = jnp.where((giver == sequence[0]) | (receiver == sequence[0]) | (lengths[receiver] == 0), 0, jnp.maximum(slack, 0))
    moved = jax.random.randint(jax.random.fold_in(own, 4), (count // 2,), 0, 1 << 20) % (slack + 1)
    lengths = lengths.at[giver].add(-moved).at[receiver].add(moved)
    labels = jnp.searchsorted(jnp.cumsum(lengths), jnp.arange(rows * top), side="right").astype(jnp.int32)
    table = labels.reshape(top, rows).T
    table = table[jax.random.permutation(jax.random.fold_in(own, 1), rows)]
    turn = jax.random.randint(jax.random.fold_in(own, 2), (rows, 1), 0, top)
    return jnp.take_along_axis(table, (jnp.arange(top)[None, :] + turn) % top, axis=1)


def shares(number_of, total, limit, lean, full):
    weights = [(1 << 20) // math.isqrt(grade ** lean) + 1 for grade in range(1, number_of + 1)]
    largest = limit if full else min(limit, max(-(-total // number_of), total * weights[0] // sum(weights)))
    least = 1 if total - largest >= number_of - 1 else 0
    counts, rest = [largest] + [least] * (number_of - 1), total - largest - least * (number_of - 1)
    while rest > 0:
        free = [i for i in range(1, number_of) if counts[i] < largest] or [i for i in range(1, number_of) if counts[i] < limit]
        whole, left = sum([weights[i] for i in free]), rest
        for i in free:
            more = min(limit - counts[i], max(1, left * weights[i] // whole), rest)
            counts[i] = counts[i] + more
            rest = rest - more
    return np.array(counts)


def setup_inputs(seed: int = 0) -> dict:
    key_list = jax.random.split(jax.random.key(seed), 9)
    thermal_profile = jnp.clip(0.6 + 0.79999995 * jax.random.uniform(key_list[0], (HEIGHT_LAYERS, TOTAL_PROFILES), jnp.float32) ** levels(key_list[0], (HEIGHT_LAYERS, TOTAL_PROFILES), ((1, 128),), -0.2, 0.2), 0.6, 1.4)
    gas_loadings = jnp.clip(jnp.exp(math.log(2.0) - 3.6888794 * jax.random.uniform(key_list[1], (NABS, HEIGHT_LAYERS, TOTAL_PROFILES), jnp.float32) ** levels(key_list[1], (NABS, HEIGHT_LAYERS, TOTAL_PROFILES), ((2, 128),), -0.2, 0.2)), 0.05, 2.0)
    profile_footprint = jnp.clip(jnp.exp(math.log(4.0) - 1.3862944 * jax.random.uniform(key_list[2], (TOTAL_PROFILES,), jnp.float32) ** levels(key_list[2], (TOTAL_PROFILES,), ((0, 128),), -0.2, 0.2)), 1.0, 4.0)
    profile_segment = place_ends(jax.random.randint(key_list[3], (TOTAL_PROFILES,), 0, P_DEV), jax.random.fold_in(key_list[3], 1), 0, P_DEV - 1).astype(jnp.int32)
    segment_holder_chip_keys = jax.random.split(jax.random.fold_in(key_list[4], 1), NPIECE // P_DEV)
    segment_holder_chip_turns = jax.random.permutation(jax.random.fold_in(key_list[4], 3), NPIECE // P_DEV)
    segment_holder_chip = jax.vmap(lambda own, number: deal_out(jax.random.fold_in(key_list[4], 2), own, number, P_DEV, DEVICES, 1, CAP, 2))(segment_holder_chip_keys, segment_holder_chip_turns).reshape((NPIECE, 1))
    segment_box_local = place_ends(jax.random.randint(key_list[5], (NPIECE,), 0, C_DEV), jax.random.fold_in(key_list[5], 1), 0, C_DEV - 1).astype(jnp.int32)
    opacity_table = jnp.clip(jnp.exp(jax.random.uniform(key_list[6], (G, NABS), jnp.float32, math.log(0.002), math.log(0.5))), 0.002, 0.5)
    blackbody_fraction = jnp.clip(jnp.exp(jax.random.uniform(key_list[7], (G,), jnp.float32, math.log(0.02), math.log(0.1))), 0.02, 0.1)
    return {"thermal_profile": thermal_profile, "gas_loadings": gas_loadings, "profile_footprint": profile_footprint, "profile_segment": profile_segment, "segment_holder_chip": segment_holder_chip, "segment_box_local": segment_box_local, "opacity_table": opacity_table, "blackbody_fraction": blackbody_fraction}


def radiate(fields, opacity_table, blackbody_fraction, layer_sequence):
    count = fields.shape[1]
    temp_rows = fields[:layer_sequence]
    absorb = fields[layer_sequence:].reshape(-1, layer_sequence, count)
    depth = jnp.einsum("ga,alc->lgc", opacity_table, absorb, precision=lax.Precision.HIGHEST)
    trans = jnp.exp(-depth)
    source = blackbody_fraction[None, :, None] * (temp_rows ** 4)[:, None, :]
    emitted = (1.0 - trans) * source

    def advance(flux, inputs):
        new_flux = inputs[0] * flux + inputs[1]
        return new_flux, jnp.sum(new_flux, axis=0)

    start = jnp.zeros((opacity_table.shape[0], count), jnp.float32)
    bottom, lower_sum = lax.scan(advance, start, (trans, emitted), unroll=8)
    surface = 0.95 * source[layer_sequence - 1] + 0.05 * bottom
    _, upper_sum = lax.scan(advance, surface, (trans, emitted), reverse=True, unroll=8)
    down_all = jnp.concatenate([jnp.zeros((1, count), jnp.float32), lower_sum], 0)
    up_all = jnp.concatenate([upper_sum, jnp.sum(surface, axis=0)[None]], 0)
    net = up_all - down_all
    return net[1:] - net[:-1]


def reference(thermal_profile, gas_loadings, profile_footprint, profile_segment, segment_holder_chip, segment_box_local, opacity_table, blackbody_fraction):
    variable_records = (NABS + 1) * HEIGHT_LAYERS
    profile_records = jnp.concatenate([thermal_profile[None], gas_loadings], 0).reshape(variable_records, TOTAL_PROFILES)
    owner_fine = jnp.arange(TOTAL_PROFILES, dtype=jnp.int32) // F_DEV
    global_piece = (owner_fine * P_DEV + profile_segment).astype(jnp.int32)
    global_cell = (segment_holder_chip[:, 0] * C_DEV + segment_box_local).astype(jnp.int32)
    cell_fine = global_cell[global_piece]
    weighted = (profile_records * profile_footprint[None, :]).T
    sums = jax.ops.segment_sum(weighted, cell_fine, num_segments=NCOARSE)
    weight = jax.ops.segment_sum(profile_footprint, cell_fine, num_segments=NCOARSE)
    cell_mean = sums / jnp.maximum(weight, 1.0)[:, None]
    blocks = cell_mean.reshape(DEVICES, C_DEV, variable_records)

    def block_heat(block):
        return radiate(block.T, opacity_table, blackbody_fraction, HEIGHT_LAYERS)

    heat_blocks = lax.map(block_heat, blocks)
    heat_cells = jnp.transpose(heat_blocks, (1, 0, 2)).reshape(HEIGHT_LAYERS, NCOARSE)
    return heat_cells[:, cell_fine]
```

```python
import functools

import jax
import jax.numpy as jnp
from jax import lax
from jax.experimental import pallas as pl
from jax.experimental.pallas import tpu as pltpu
from jax.sharding import PartitionSpec as P

AXES = ("dyn", "rad")
CAP = 8
LANES = 128
BF = jnp.bfloat16
F32 = jnp.float32
NT = (((1,), (1,)), ((), ()))
NN = (((1,), (0,)), ((), ()))
VMEM_LIMIT = 56 * 1024 * 1024


def up_to(value, step):
    return -(-value // step) * step


def parts_of(value, count):
    out = []
    for _ in range(count - 1):
        part = value.astype(BF)
        out.append(part)
        value = value - part.astype(F32)
    out.append(value.astype(BF))
    return out


def mask_to(mask):
    return jnp.where(mask, 1.0, 0.0).astype(BF)


def dot(a, b, dims):
    return lax.dot_general(a, b, dims, preferred_element_type=F32)


def slots_of(target, devices):
    pieces = target.shape[1]
    column = jnp.transpose(jnp.broadcast_to(target, (LANES, pieces)))
    ranks = []
    for j in range(pieces // LANES):
        part = target[:, j * LANES : (j + 1) * LANES]
        before = lax.broadcasted_iota(jnp.int32, (pieces, LANES), 0)
        me = lax.broadcasted_iota(jnp.int32, (pieces, LANES), 1) + j * LANES
        hit = (column == part) & (before < me)
        ranks.append(jnp.sum(jnp.where(hit, 1, 0), axis=0, keepdims=True))
    return jnp.concatenate(ranks, axis=1)


def slot_rows(target, rank, devices, store):
    pieces = target.shape[1]
    owner = lax.broadcasted_iota(jnp.int32, (devices, pieces), 0) == target
    for s in range(CAP):
        store(s, mask_to(owner & (rank == s)))


def piece_rows(segment, pieces):
    return mask_to(lax.broadcasted_iota(jnp.int32, (pieces, segment.shape[1]), 0) == segment)


class Plan:
    def __init__(self, fields, width):
        self.fields = fields
        self.whole = fields // LANES
        self.rest = fields - self.whole * LANES
        self.width = width
        self.tail = up_to(CAP * width, LANES) // LANES
        self.rows = CAP * self.whole + self.tail

    def spans(self, s):
        start = s * self.width
        first, shift = start // LANES, start % LANES
        yield first, shift, None if shift + self.width <= LANES else "low"
        if shift + self.width > LANES:
            yield first + 1, shift, "high"

    def pack(self, rests):
        lane = lax.broadcasted_iota(jnp.int32, rests[0].shape, 1)
        tiles = [None] * self.tail
        for s, rest in enumerate(rests):
            for tile, shift, side in self.spans(s):
                part = pltpu.roll(rest, shift, 1) if shift else rest
                if side == "low":
                    part = jnp.where(lane >= shift, part, 0.0)
                if side == "high":
                    part = jnp.where(lane < shift, part, 0.0)
                tiles[tile] = part if tiles[tile] is None else tiles[tile] + part
        return tiles

    def unpack(self, tiles, s):
        spans = list(self.spans(s))
        value, shift = tiles[spans[0][0]], spans[0][1]
        if len(spans) == 2:
            lane = lax.broadcasted_iota(jnp.int32, value.shape, 1)
            value = jnp.where(lane >= shift, value, tiles[spans[1][0]])
        return pltpu.roll(value, LANES - shift, 1) if shift else value


def gather_kernel(plan, devices, thermal, gas, weight, segment, target, box, out, rank_out, buf, sems, left, ones, comp, slot, wide):
    species, levels = buf.shape[0], buf.shape[1]
    pieces = target.shape[1]
    block = up_to(levels, 16)
    copies = [pltpu.make_async_copy(thermal, buf.at[0], sems.at[0])]
    copies += [pltpu.make_async_copy(gas.at[k], buf.at[k + 1], sems.at[k + 1]) for k in range(species - 1)]
    for copy in copies:
        copy.start()
    owner = target[...]
    rank = slots_of(owner, devices)
    rank_out[...] = rank

    def store(s, value):
        slot[s * devices : (s + 1) * devices, :] = value

    slot_rows(owner, rank, devices, store)
    ones[...] = piece_rows(segment[...], pieces)
    w = weight[...]
    high, low = parts_of(jnp.broadcast_to(w, (8, w.shape[1])), 2)
    left[2 * species * block :, :] = jnp.concatenate([high.astype(F32), low.astype(F32)], axis=0).astype(BF)
    for k in range(species):
        copies[k].wait()
        high, low = parts_of(buf[k] * w, 2)
        left[k * block : k * block + levels, :] = high
        left[(species + k) * block : (species + k) * block + levels, :] = low
    sums = dot(left[...], ones[...], NT)
    for k in range(species):
        a = k * block
        b = (species + k) * block
        comp[k * levels : (k + 1) * levels, :] = sums[a : a + levels] + sums[b : b + levels]
    total = species * levels
    end = 2 * species * block
    comp[total : total + 1, :] = sums[end : end + 1] + sums[end + 8 : end + 9]
    comp[total + 1 : total + 2, :] = box[...].astype(F32)
    comp[total + 2 :, :] = jnp.zeros((comp.shape[0] - total - 2, pieces), F32)
    acc = None
    for part in parts_of(comp[...], 3):
        term = dot(slot[...], part, NT)
        acc = term if acc is None else acc + term
    wide[...] = acc
    for k in range(plan.whole):
        for s in range(CAP):
            out[pl.ds(CAP * k + s, devices, stride=plan.rows), :] = wide[
                s * devices : (s + 1) * devices, k * LANES : (k + 1) * LANES
            ]
    rests = [wide[s * devices : (s + 1) * devices, plan.whole * LANES :] for s in range(CAP)]
    for j, tile in enumerate(plan.pack(rests)):
        out[pl.ds(CAP * plan.whole + j, devices, stride=plan.rows), :] = tile


def sweep(mean, t4, opacity, fraction, heat, lost, gain, levels, cells):
    points = opacity.shape[1]
    rate = [-opacity[a] for a in range(opacity.shape[0])]
    frac = fraction[...]

    def row(ref, index):
        return ref[pl.ds(index, 1), :]

    def down(l, flux):
        tau = rate[0] * row(mean, levels + l)
        for a in range(1, len(rate)):
            tau = tau + rate[a] * row(mean, (a + 1) * levels + l)
        take = 1.0 - jnp.exp(tau)
        lost[l] = take
        step = take * (frac * row(t4, l) - flux)
        gain[l] = jnp.sum(step.reshape(points // 8, 8, cells), axis=0)
        return flux + step

    bottom = lax.fori_loop(0, levels, down, jnp.zeros((points, cells), F32), unroll=8)
    surface = 0.95 * (frac * t4[levels - 1 : levels, :]) + 0.05 * bottom

    def up(i, flux):
        l = levels - 1 - i
        step = lost[l] * (frac * row(t4, l) - flux)
        part = gain[l] + jnp.sum(step.reshape(points // 8, 8, cells), axis=0)
        heat[pl.ds(l, 1), :] = -jnp.sum(part, axis=0, keepdims=True)
        return flux + step

    lax.fori_loop(0, levels, up, surface, unroll=8)


def radiate_kernel(plan, back, devices, levels, cells, arrived, opacity, fraction, out, parts, match, mean, t4, heat, lost, gain):
    fields = plan.fields
    lane = plan.rest
    tails = [arrived[pl.ds(CAP * plan.whole + j, devices, stride=plan.rows), :] for j in range(plan.tail)]
    pick = mask_to(lax.broadcasted_iota(jnp.int32, (8, LANES), 1) == lane - 1)
    rows = []
    for s in range(CAP):
        own = slice(s * devices, (s + 1) * devices)
        for k in range(plan.whole):
            value = arrived[pl.ds(CAP * k + s, devices, stride=plan.rows), :]
            for n, part in enumerate(parts_of(value, 3)):
                parts[n, own, k * LANES : (k + 1) * LANES] = part
        rest = plan.unpack(tails, s)
        split = parts_of(rest, 3)
        for n, part in enumerate(split):
            parts[n, own, plan.whole * LANES :] = part
        cell = rest[:, lane - 1 : lane].astype(jnp.int32)
        match[own, :] = mask_to(cell == lax.broadcasted_iota(jnp.int32, (devices, cells), 1))
        rows.append(dot(pick, split[0], NT)[0:1])
    cell_row = jnp.concatenate(rows, axis=1).astype(jnp.int32)
    slots = cell_row.shape[1]
    turned = mask_to(lax.broadcasted_iota(jnp.int32, (cells, slots), 0) == cell_row)
    acc = None
    for n in range(3):
        term = dot(turned, parts[n], NN)
        acc = term if acc is None else acc + term
    sums = jnp.transpose(acc)
    weight = sums[fields - 2 : fields - 1, :]
    mean[...] = sums[0 : mean.shape[0]] * (1.0 / jnp.maximum(weight, 1.0))
    square = mean[0:levels, :] * mean[0:levels, :]
    t4[0:levels, :] = square * square
    heat[levels:, :] = jnp.zeros((heat.shape[0] - levels, cells), F32)
    sweep(mean, t4, opacity, fraction, heat, lost, gain, levels, cells)
    acc = None
    for part in parts_of(heat[...], 3):
        term = dot(match[...], part, NT)
        acc = term if acc is None else acc + term
    for s in range(CAP):
        out[pl.ds(s, devices, stride=back.rows), :] = acc[s * devices : (s + 1) * devices, :LANES]
    rests = [acc[s * devices : (s + 1) * devices, LANES:] for s in range(CAP)]
    for j, tile in enumerate(back.pack(rests)):
        out[pl.ds(CAP + j, devices, stride=back.rows), :] = tile


def spread_kernel(back, devices, levels, returned, segment, target, rank, out, slot, wide):
    pieces = target.shape[1]

    def store(s, value):
        slot[s * devices : (s + 1) * devices, :] = value

    slot_rows(target[...], rank[...], devices, store)
    ones = piece_rows(segment[...], pieces)
    tails = [returned[pl.ds(CAP + j, devices, stride=back.rows), :] for j in range(back.tail)]
    for s in range(CAP):
        own = slice(s * devices, (s + 1) * devices)
        wide[own, :LANES] = returned[pl.ds(s, devices, stride=back.rows), :]
        wide[own, LANES:] = back.unpack(tails, s)
    turned = jnp.transpose(wide[...])[: up_to(levels, 16)]
    held = None
    for part in parts_of(turned, 3):
        term = dot(part, slot[...], NN)
        held = term if held is None else held + term
    acc = None
    for part in parts_of(held, 3):
        term = dot(part, ones, NN)
        acc = term if acc is None else acc + term
    out[...] = acc[:levels]


def shards(thermal, gas, footprint, segment, holder, box, opacity, fraction):
    levels, columns = thermal.shape
    species = gas.shape[0] + 1
    pieces = box.shape[0]
    points = fraction.shape[0]
    devices = lax.axis_size(AXES)
    cells = columns // 8
    slots = devices * CAP
    fields = species * levels + 2
    plan = Plan(fields, up_to(fields % LANES, 16))
    back = Plan(levels, up_to(levels % LANES, 16))
    padded = (plan.whole + 1) * LANES
    block = up_to(levels, 16)
    weight_row = footprint.reshape(1, columns)
    segment_row = segment.reshape(1, columns)
    target_row = holder.reshape(1, pieces)
    box_row = box.reshape(1, pieces)
    vmem = pl.BlockSpec(memory_space=pltpu.VMEM)
    hbm = pl.BlockSpec(memory_space=pl.ANY)
    params = pltpu.CompilerParams(vmem_limit_bytes=VMEM_LIMIT)

    outgoing, rank = pl.pallas_call(
        functools.partial(gather_kernel, plan, devices),
        out_shape=(
            jax.ShapeDtypeStruct((devices * plan.rows, LANES), F32),
            jax.ShapeDtypeStruct((1, pieces), jnp.int32),
        ),
        in_specs=[hbm, hbm, vmem, vmem, vmem, vmem],
        out_specs=(vmem, vmem),
        scratch_shapes=[
            pltpu.VMEM((species, levels, columns), F32),
            pltpu.SemaphoreType.DMA((species,)),
            pltpu.VMEM((2 * species * block + 16, columns), BF),
            pltpu.VMEM((pieces, columns), BF),
            pltpu.VMEM((padded, pieces), F32),
            pltpu.VMEM((slots, pieces), BF),
            pltpu.VMEM((slots, padded), F32),
        ],
        compiler_params=params,
        name="gather_pieces",
    )(thermal, gas, weight_row, segment_row, target_row, box_row)

    arrived = lax.all_to_all(
        outgoing.reshape(devices, 1, plan.rows * LANES), AXES, split_axis=0, concat_axis=0, tiled=True
    ).reshape(devices * plan.rows, LANES)

    heat_out = pl.pallas_call(
        functools.partial(radiate_kernel, plan, back, devices, levels, cells),
        out_shape=jax.ShapeDtypeStruct((devices * back.rows, LANES), F32),
        in_specs=[vmem, vmem, vmem],
        out_specs=vmem,
        scratch_shapes=[
            pltpu.VMEM((3, slots, padded), BF),
            pltpu.VMEM((slots, cells), BF),
            pltpu.VMEM((up_to(species * levels, 8), cells), F32),
            pltpu.VMEM((up_to(levels, 8), cells), F32),
            pltpu.VMEM((2 * LANES, cells), F32),
            pltpu.VMEM((levels, points, cells), F32),
            pltpu.VMEM((levels, 8, cells), F32),
        ],
        compiler_params=params,
        name="radiate_cells",
    )(
        arrived,
        jnp.broadcast_to(opacity.T[:, :, None], (species - 1, points, cells)),
        jnp.broadcast_to(fraction[:, None], (points, cells)),
    )

    returned = lax.all_to_all(
        heat_out.reshape(devices, 1, back.rows * LANES), AXES, split_axis=0, concat_axis=0, tiled=True
    ).reshape(devices * back.rows, LANES)

    return pl.pallas_call(
        functools.partial(spread_kernel, back, devices, levels),
        out_shape=jax.ShapeDtypeStruct((levels, columns), F32),
        in_specs=[vmem, vmem, vmem, vmem],
        out_specs=vmem,
        scratch_shapes=[
            pltpu.VMEM((slots, pieces), BF),
            pltpu.VMEM((slots, 2 * LANES), F32),
        ],
        compiler_params=params,
        name="spread_heat",
    )(returned, segment_row, target_row, rank)


def solution(mesh):
    placed = (
        P(None, AXES),
        P(None, None, AXES),
        P(AXES),
        P(AXES),
        P(AXES, None),
        P(AXES),
        P(),
        P(),
    )
    return jax.shard_map(shards, mesh=mesh, in_specs=placed, out_specs=P(None, AXES), check_vma=False)
```

```python
import functools

import jax
import jax.numpy as jnp
from jax import lax
from jax.experimental import pallas as pl
from jax.experimental.pallas import tpu as pltpu
from jax.sharding import PartitionSpec as P

AXES = ("dyn", "rad")
CAP = 8
LANES = 128
BF = jnp.bfloat16
F32 = jnp.float32
NT = (((1,), (1,)), ((), ()))
NN = (((1,), (0,)), ((), ()))
MIB = 1024 * 1024


def up_to(value, step):
    return -(-value // step) * step


def parts_of(value, count):
    out = []
    for _ in range(count - 1):
        part = value.astype(BF)
        out.append(part)
        value = value - part.astype(F32)
    out.append(value.astype(BF))
    return out


def mask_to(mask):
    return jnp.where(mask, 1.0, 0.0).astype(BF)


def dot(a, b, dims):
    return lax.dot_general(a, b, dims, preferred_element_type=F32)


def slots_of(target, devices):
    pieces = target.shape[1]
    column = jnp.transpose(jnp.broadcast_to(target, (LANES, pieces)))
    ranks = []
    for j in range(pieces // LANES):
        part = target[:, j * LANES : (j + 1) * LANES]
        before = lax.broadcasted_iota(jnp.int32, (pieces, LANES), 0)
        me = lax.broadcasted_iota(jnp.int32, (pieces, LANES), 1) + j * LANES
        hit = (column == part) & (before < me)
        ranks.append(jnp.sum(jnp.where(hit, 1, 0), axis=0, keepdims=True))
    return jnp.concatenate(ranks, axis=1)


def slot_rows(target, rank, devices, store):
    pieces = target.shape[1]
    owner = lax.broadcasted_iota(jnp.int32, (devices, pieces), 0) == target
    for s in range(CAP):
        store(s, mask_to(owner & (rank == s)))


def piece_rows(segment, pieces):
    return mask_to(lax.broadcasted_iota(jnp.int32, (pieces, segment.shape[1]), 0) == segment)


class Plan:
    def __init__(self, fields, width):
        self.fields = fields
        self.whole = fields // LANES
        self.rest = fields - self.whole * LANES
        self.width = width
        self.tail = up_to(CAP * width, LANES) // LANES
        self.rows = CAP * self.whole + self.tail

    def spans(self, s):
        start = s * self.width
        first, shift = start // LANES, start % LANES
        yield first, shift, None if shift + self.width <= LANES else "low"
        if shift + self.width > LANES:
            yield first + 1, shift, "high"

    def pack(self, rests):
        lane = lax.broadcasted_iota(jnp.int32, rests[0].shape, 1)
        tiles = [None] * self.tail
        for s, rest in enumerate(rests):
            for tile, shift, side in self.spans(s):
                part = pltpu.roll(rest, shift, 1) if shift else rest
                if side == "low":
                    part = jnp.where(lane >= shift, part, 0.0)
                if side == "high":
                    part = jnp.where(lane < shift, part, 0.0)
                tiles[tile] = part if tiles[tile] is None else tiles[tile] + part
        return tiles

    def unpack(self, tiles, s):
        spans = list(self.spans(s))
        value, shift = tiles[spans[0][0]], spans[0][1]
        if len(spans) == 2:
            lane = lax.broadcasted_iota(jnp.int32, value.shape, 1)
            value = jnp.where(lane >= shift, value, tiles[spans[1][0]])
        return pltpu.roll(value, LANES - shift, 1) if shift else value


def gather_kernel(plan, devices, groups, thermal, gas, weight_in, segment_in, target_in, box_in, out, rank_out, buf, sems, weight, segment, target, box, left, ones, comp, slot):
    species, levels, columns = buf.shape
    pieces = target.shape[1]
    block = up_to(levels, 16)
    small = [(target_in, target), (segment_in, segment), (weight_in, weight), (box_in, box)]
    rows = [pltpu.make_async_copy(a, b, sems.at[species + n]) for n, (a, b) in enumerate(small)]
    for copy in rows:
        copy.start()
    copies = [pltpu.make_async_copy(thermal, buf.at[0], sems.at[0])]
    copies += [pltpu.make_async_copy(gas.at[:, k, :], buf.at[k + 1], sems.at[k + 1]) for k in range(species - 1)]
    for copy in copies:
        copy.start()
    rows[0].wait()
    owner = target[...]
    rank = slots_of(owner, devices)
    rank_out[...] = rank

    def store(s, value):
        for n in range(2):
            slot[s * devices : (s + 1) * devices, n * pieces : (n + 1) * pieces] = value

    slot_rows(owner, rank, devices, store)
    rows[1].wait()
    here = piece_rows(segment[...], pieces)
    for n in range(2):
        ones[:, n * columns : (n + 1) * columns] = here
    rows[2].wait()
    rows[3].wait()
    w = weight[...]
    end = species * block
    for n, part in enumerate(parts_of(jnp.broadcast_to(w, (16, columns)), 2)):
        left[end:, n * columns : (n + 1) * columns] = part
    total = species * levels
    begin = 0
    for group in groups:
        for k in range(begin, begin + group):
            copies[k].wait()
            for n, part in enumerate(parts_of(buf[k] * w, 2)):
                left[k * block : k * block + levels, n * columns : (n + 1) * columns] = part
        stop = begin + group
        last = stop == species
        sums = dot(left[begin * block : left.shape[0] if last else stop * block, :], ones[...], NT)
        for k in range(begin, stop):
            a = (k - begin) * block
            for n, part in enumerate(parts_of(sums[a : a + levels], 2)):
                comp[k * levels : (k + 1) * levels, n * pieces : (n + 1) * pieces] = part
        if last:
            a = (stop - begin) * block
            row = lax.broadcasted_iota(jnp.int32, (comp.shape[0] - total, pieces), 0)
            rest = jnp.where(row == 0, sums[a : a + 1], jnp.where(row == 1, box[...].astype(F32), 0.0))
            for n, part in enumerate(parts_of(rest, 2)):
                comp[total:, n * pieces : (n + 1) * pieces] = part
        begin = stop
    wide = 2 * LANES
    for k in range(comp.shape[0] // wide):
        acc = dot(slot[...], comp[k * wide : (k + 1) * wide, :], NT)
        for h in range(2):
            tile = 2 * k + h
            values = [acc[s * devices : (s + 1) * devices, h * LANES : (h + 1) * LANES] for s in range(CAP)]
            if tile < plan.whole:
                for s in range(CAP):
                    out[pl.ds(CAP * tile + s, devices, stride=plan.rows), :] = values[s]
            else:
                for j, value in enumerate(plan.pack(values)):
                    out[pl.ds(CAP * tile + j, devices, stride=plan.rows), :] = value


def as_column(row, width):
    n = row.shape[1]
    same = lax.broadcasted_iota(jnp.int32, (n, n), 0) == lax.broadcasted_iota(jnp.int32, (n, n), 1)
    return jnp.broadcast_to(jnp.sum(jnp.where(same, row, 0.0), axis=1, keepdims=True), (n, width))


def sweep(mean, t4, rate, frac, heat, lost, gain, levels, cells):
    points = frac.shape[0]

    def row(ref, index):
        return ref[pl.ds(index, 1), :]

    def down(l, flux):
        tau = rate[0] * row(mean, levels + l)
        for a in range(1, len(rate)):
            tau = tau + rate[a] * row(mean, (a + 1) * levels + l)
        take = 1.0 - jnp.exp(tau)
        lost[l] = take
        step = take * (frac * row(t4, l) - flux)
        gain[l] = jnp.sum(step.reshape(points // 8, 8, cells), axis=0)
        return flux + step

    bottom = lax.fori_loop(0, levels, down, jnp.zeros((points, cells), F32), unroll=8)
    surface = 0.95 * (frac * t4[levels - 1 : levels, :]) + 0.05 * bottom

    def up(i, flux):
        l = levels - 1 - i
        step = lost[l] * (frac * row(t4, l) - flux)
        part = gain[l] + jnp.sum(step.reshape(points // 8, 8, cells), axis=0)
        heat[pl.ds(l, 1), :] = -jnp.sum(part, axis=0, keepdims=True)
        return flux + step

    lax.fori_loop(0, levels, up, surface, unroll=8)


def radiate_kernel(plan, back, devices, levels, cells, arrived, opacity_in, fraction_in, out, opacity, fraction, sems, parts, match, mean, t4, heat, lost, gain):
    copies = [
        pltpu.make_async_copy(opacity_in, opacity, sems.at[0]),
        pltpu.make_async_copy(fraction_in, fraction, sems.at[1]),
    ]
    for copy in copies:
        copy.start()
    fields = plan.fields
    lane = plan.rest
    tails = [arrived[pl.ds(CAP * plan.whole + j, devices, stride=plan.rows), :] for j in range(plan.tail)]
    pick = mask_to(lax.broadcasted_iota(jnp.int32, (8, LANES), 1) == lane - 1)
    rows = []
    for s in range(CAP):
        own = slice(s * devices, (s + 1) * devices)
        for k in range(plan.whole):
            value = arrived[pl.ds(CAP * k + s, devices, stride=plan.rows), :]
            for n, part in enumerate(parts_of(value, 3)):
                parts[n, own, k * LANES : (k + 1) * LANES] = part
        rest = plan.unpack(tails, s)
        split = parts_of(rest, 3)
        for n, part in enumerate(split):
            parts[n, own, plan.whole * LANES :] = part
        cell = rest[:, lane - 1 : lane].astype(jnp.int32)
        match[own, :] = mask_to(cell == lax.broadcasted_iota(jnp.int32, (devices, cells), 1))
        rows.append(dot(pick, split[0], NT)[0:1])
    cell_row = jnp.concatenate(rows, axis=1).astype(jnp.int32)
    slots = cell_row.shape[1]
    turned = mask_to(lax.broadcasted_iota(jnp.int32, (cells, slots), 0) == cell_row)
    acc = None
    for n in range(3):
        term = dot(turned, parts[n], NN)
        acc = term if acc is None else acc + term
    sums = jnp.transpose(acc)
    weight = sums[fields - 2 : fields - 1, :]
    mean[...] = sums[0 : mean.shape[0]] * (1.0 / jnp.maximum(weight, 1.0))
    square = mean[0:levels, :] * mean[0:levels, :]
    t4[0:levels, :] = square * square
    heat[levels:, :] = jnp.zeros((heat.shape[0] - levels, cells), F32)
    for copy in copies:
        copy.wait()
    rate = [as_column(-opacity[a : a + 1, :], cells) for a in range(opacity.shape[0])]
    frac = as_column(fraction[...], cells)
    sweep(mean, t4, rate, frac, heat, lost, gain, levels, cells)
    acc = None
    for part in parts_of(heat[...], 3):
        term = dot(match[...], part, NT)
        acc = term if acc is None else acc + term
    for s in range(CAP):
        out[pl.ds(s, devices, stride=back.rows), :] = acc[s * devices : (s + 1) * devices, :LANES]
    rests = [acc[s * devices : (s + 1) * devices, LANES:] for s in range(CAP)]
    for j, tile in enumerate(back.pack(rests)):
        out[pl.ds(CAP + j, devices, stride=back.rows), :] = tile


def spread_kernel(back, devices, levels, returned, segment, target, rank, out, slot, wide):
    pieces = target.shape[1]

    def store(s, value):
        slot[s * devices : (s + 1) * devices, :] = value

    slot_rows(target[...], rank[...], devices, store)
    ones = piece_rows(segment[...], pieces)
    tails = [returned[pl.ds(CAP + j, devices, stride=back.rows), :] for j in range(back.tail)]
    for s in range(CAP):
        own = slice(s * devices, (s + 1) * devices)
        wide[own, :LANES] = returned[pl.ds(s, devices, stride=back.rows), :]
        wide[own, LANES:] = back.unpack(tails, s)
    turned = jnp.transpose(wide[...])[: up_to(levels, 16)]
    held = None
    for part in parts_of(turned, 3):
        term = dot(part, slot[...], NN)
        held = term if held is None else held + term
    acc = None
    for part in parts_of(held, 3):
        term = dot(part, ones, NN)
        acc = term if acc is None else acc + term
    out[...] = acc[:levels]


VMEM = pl.BlockSpec(memory_space=pltpu.VMEM)
HBM = pl.BlockSpec(memory_space=pl.ANY)


def params(mib):
    return pltpu.CompilerParams(vmem_limit_bytes=mib * MIB)


def in_hbm(value):
    return pltpu.with_memory_space_constraint(value, pltpu.HBM)


def plans(levels, species):
    fields = species * levels + 2
    return Plan(fields, up_to(fields % LANES, 16)), Plan(levels, up_to(levels % LANES, 16))


def gather_call(thermal, gas, weight_row, segment_row, target_row, box_row):
    levels, columns = thermal.shape
    species = gas.shape[1] + 1
    pieces = target_row.shape[1]
    devices = lax.axis_size(AXES)
    plan, _ = plans(levels, species)
    padded = (plan.whole + 1) * LANES
    slots = devices * CAP
    return pl.pallas_call(
        functools.partial(gather_kernel, plan, devices, (3, 2)),
        out_shape=(
            jax.ShapeDtypeStruct((devices * plan.rows, LANES), F32),
            jax.ShapeDtypeStruct((1, pieces), jnp.int32),
        ),
        in_specs=[HBM] * 6,
        out_specs=(VMEM, VMEM),
        scratch_shapes=[
            pltpu.VMEM((species, levels, columns), F32),
            pltpu.SemaphoreType.DMA((species + 4,)),
            pltpu.VMEM((1, columns), F32),
            pltpu.VMEM((1, columns), jnp.int32),
            pltpu.VMEM((1, pieces), jnp.int32),
            pltpu.VMEM((1, pieces), jnp.int32),
            pltpu.VMEM((species * up_to(levels, 16) + 16, 2 * columns), BF),
            pltpu.VMEM((pieces, 2 * columns), BF),
            pltpu.VMEM((padded, 2 * pieces), BF),
            pltpu.VMEM((slots, 2 * pieces), BF),
        ],
        compiler_params=params(34),
        name="gather_pieces",
    )(*map(in_hbm, (thermal, gas, weight_row, segment_row, target_row, box_row)))


def radiate_call(arrived, opacity, fraction, levels, cells):
    absorbers, points = opacity.shape
    species = absorbers + 1
    devices = lax.axis_size(AXES)
    plan, back = plans(levels, species)
    padded = (plan.whole + 1) * LANES
    slots = devices * CAP
    return pl.pallas_call(
        functools.partial(radiate_kernel, plan, back, devices, levels, cells),
        out_shape=jax.ShapeDtypeStruct((devices * back.rows, LANES), F32),
        in_specs=[VMEM, HBM, HBM],
        out_specs=VMEM,
        scratch_shapes=[
            pltpu.VMEM((absorbers, points), F32),
            pltpu.VMEM((1, points), F32),
            pltpu.SemaphoreType.DMA((2,)),
            pltpu.VMEM((3, slots, padded), BF),
            pltpu.VMEM((slots, cells), BF),
            pltpu.VMEM((up_to(species * levels, 8), cells), F32),
            pltpu.VMEM((up_to(levels, 8), cells), F32),
            pltpu.VMEM((2 * LANES, cells), F32),
            pltpu.VMEM((levels, points, cells), F32),
            pltpu.VMEM((levels, 8, cells), F32),
        ],
        compiler_params=params(28),
        name="radiate_cells",
    )(arrived, in_hbm(opacity), in_hbm(fraction))


def spread_call(returned, segment_row, target_row, rank, levels):
    columns = segment_row.shape[1]
    pieces = target_row.shape[1]
    devices = lax.axis_size(AXES)
    _, back = plans(levels, 1)
    slots = devices * CAP
    return pl.pallas_call(
        functools.partial(spread_kernel, back, devices, levels),
        out_shape=jax.ShapeDtypeStruct((levels, columns), F32),
        in_specs=[VMEM, VMEM, VMEM, VMEM],
        out_specs=VMEM,
        scratch_shapes=[
            pltpu.VMEM((slots, pieces), BF),
            pltpu.VMEM((slots, 2 * LANES), F32),
        ],
        compiler_params=params(20),
        name="spread_heat",
    )(returned, segment_row, target_row, rank)


def exchange(value):
    devices = lax.axis_size(AXES)
    chunks = value.reshape(devices, 1, value.size // devices)
    return lax.all_to_all(chunks, AXES, split_axis=0, concat_axis=0, tiled=True).reshape(value.shape)


def shards(thermal, gas, footprint, segment, holder, box, opacity, fraction):
    levels, columns = thermal.shape
    pieces = box.shape[0]
    segment_row = segment.reshape(1, columns)
    target_row = holder.reshape(1, pieces)
    outgoing, rank = gather_call(
        thermal, gas.transpose(1, 0, 2), footprint.reshape(1, columns), segment_row, target_row, box.reshape(1, pieces)
    )
    arrived = exchange(outgoing)
    heat = radiate_call(arrived, opacity.T, fraction.reshape(1, -1), levels, columns // 8)
    returned = exchange(heat)
    return spread_call(returned, segment_row, target_row, rank, levels)


def solution(mesh):
    placed = (
        P(None, AXES),
        P(None, None, AXES),
        P(AXES),
        P(AXES),
        P(AXES, None),
        P(AXES),
        P(),
        P(),
    )
    return jax.shard_map(shards, mesh=mesh, in_specs=placed, out_specs=P(None, AXES), check_vma=False)
```

```python
import functools

import jax
import jax.numpy as jnp
from jax import lax
from jax.experimental import pallas as pl
from jax.experimental.pallas import tpu as pltpu
from jax.sharding import PartitionSpec as P

AXES = ("dyn", "rad")
CAP = 8
LANES = 128
BF = jnp.bfloat16
F32 = jnp.float32
NT = (((1,), (1,)), ((), ()))
NN = (((1,), (0,)), ((), ()))
MIB = 1024 * 1024
LEVELS = 16
LOG2E = 1.4426950408889634


def up_to(value, step):
    return -(-value // step) * step


def parts_of(value, count):
    out = []
    for _ in range(count - 1):
        part = value.astype(BF)
        out.append(part)
        value = value - part.astype(F32)
    out.append(value.astype(BF))
    return out


def mask_to(mask):
    return jnp.where(mask, 1.0, 0.0).astype(BF)


def dot(a, b, dims):
    return lax.dot_general(a, b, dims, preferred_element_type=F32)


def slots_of(target, devices):
    pieces = target.shape[1]
    column = jnp.transpose(jnp.broadcast_to(target, (LANES, pieces)))
    ranks = []
    for j in range(pieces // LANES):
        part = target[:, j * LANES : (j + 1) * LANES]
        before = lax.broadcasted_iota(jnp.int32, (pieces, LANES), 0)
        me = lax.broadcasted_iota(jnp.int32, (pieces, LANES), 1) + j * LANES
        hit = (column == part) & (before < me)
        ranks.append(jnp.sum(jnp.where(hit, 1, 0), axis=0, keepdims=True))
    return jnp.concatenate(ranks, axis=1)


def slot_rows(target, rank, devices, store):
    pieces = target.shape[1]
    owner = lax.broadcasted_iota(jnp.int32, (devices, pieces), 0) == target
    for s in range(CAP):
        store(s, mask_to(owner & (rank == s)))


def piece_rows(segment, pieces):
    return mask_to(lax.broadcasted_iota(jnp.int32, (pieces, segment.shape[1]), 0) == segment)


class Plan:
    def __init__(self, fields, width):
        self.fields = fields
        self.whole = fields // LANES
        self.rest = fields - self.whole * LANES
        self.width = width
        self.tail = up_to(CAP * width, LANES) // LANES
        self.rows = CAP * self.whole + self.tail

    def spans(self, s):
        start = s * self.width
        first, shift = start // LANES, start % LANES
        yield first, shift, None if shift + self.width <= LANES else "low"
        if shift + self.width > LANES:
            yield first + 1, shift, "high"

    def pack(self, rests):
        lane = lax.broadcasted_iota(jnp.int32, rests[0].shape, 1)
        tiles = [None] * self.tail
        for s, rest in enumerate(rests):
            for tile, shift, side in self.spans(s):
                part = pltpu.roll(rest, shift, 1) if shift else rest
                if side == "low":
                    part = jnp.where(lane >= shift, part, 0.0)
                if side == "high":
                    part = jnp.where(lane < shift, part, 0.0)
                tiles[tile] = part if tiles[tile] is None else tiles[tile] + part
        return tiles

    def unpack(self, tiles, s):
        spans = list(self.spans(s))
        value, shift = tiles[spans[0][0]], spans[0][1]
        if len(spans) == 2:
            lane = lax.broadcasted_iota(jnp.int32, value.shape, 1)
            value = jnp.where(lane >= shift, value, tiles[spans[1][0]])
        return pltpu.roll(value, LANES - shift, 1) if shift else value


def gather_kernel(plan, devices, groups, thermal, gas, weight_in, segment_in, target_in, box_in, out, ones, slot, buf, sems, weight, segment, target, box, left, comp):
    species, levels, columns = buf.shape
    pieces = target.shape[1]
    block = up_to(levels, 16)
    small = [(target_in, target), (segment_in, segment), (weight_in, weight), (box_in, box)]
    rows = [pltpu.make_async_copy(a, b, sems.at[species + n]) for n, (a, b) in enumerate(small)]
    for copy in rows:
        copy.start()
    copies = [pltpu.make_async_copy(thermal, buf.at[0], sems.at[0])]
    copies += [pltpu.make_async_copy(gas.at[:, k, :], buf.at[k + 1], sems.at[k + 1]) for k in range(species - 1)]
    for copy in copies:
        copy.start()
    rows[0].wait()
    owner = target[...]
    rank = slots_of(owner, devices)

    def store(s, value):
        slot[s * devices : (s + 1) * devices, :] = value

    slot_rows(owner, rank, devices, store)
    rows[1].wait()
    ones[...] = piece_rows(segment[...], pieces)
    rows[2].wait()
    rows[3].wait()
    w = weight[...]
    total = species * levels
    end = 2 * species * block
    pair = parts_of(jnp.broadcast_to(w, (8, columns)), 2)
    left[end:, :] = jnp.concatenate([part.astype(F32) for part in pair], axis=0).astype(BF)

    def load(k):
        copies[k].wait()
        for n, part in enumerate(parts_of(buf[k] * w, 2)):
            left[(2 * k + n) * block : (2 * k + n) * block + levels, :] = part

    def keep(first, rows, values):
        for n, part in enumerate(parts_of(values, 2)):
            comp[first : first + rows, n * pieces : (n + 1) * pieces] = part

    bounds = [sum(groups[:n]) for n in range(len(groups) + 1)]
    for begin, stop in zip(bounds, bounds[1:]):
        last = stop == species
        for k in range(begin, stop):
            load(k)
        sums = dot(left[2 * begin * block : end + 16 if last else 2 * stop * block, :], ones[...], NT)
        for k in range(begin, stop):
            a = 2 * (k - begin) * block
            keep(k * levels, levels, sums[a : a + levels] + sums[a + block : a + block + levels])
        if last:
            a = 2 * (stop - begin) * block
            row = lax.broadcasted_iota(jnp.int32, (comp.shape[0] - total, pieces), 0)
            held = sums[a : a + 1] + sums[a + 8 : a + 9]
            keep(total, comp.shape[0] - total, jnp.where(row == 0, held, jnp.where(row == 1, box[...].astype(F32), 0.0)))
    wide = 2 * LANES
    for k in range(comp.shape[0] // wide):
        pair = [comp[k * wide : (k + 1) * wide, n * pieces : (n + 1) * pieces] for n in range(2)]
        acc = dot(slot[...], pair[0], NT) + dot(slot[...], pair[1], NT)
        for h in range(2):
            tile = 2 * k + h
            values = [acc[s * devices : (s + 1) * devices, h * LANES : (h + 1) * LANES] for s in range(CAP)]
            if tile < plan.whole:
                for s in range(CAP):
                    out[pl.ds(CAP * tile + s, devices, stride=plan.rows), :] = values[s]
            else:
                for j, value in enumerate(plan.pack(values)):
                    out[pl.ds(CAP * tile + j, devices, stride=plan.rows), :] = value


def as_column(row, width):
    n = row.shape[1]
    same = lax.broadcasted_iota(jnp.int32, (n, n), 0) == lax.broadcasted_iota(jnp.int32, (n, n), 1)
    return jnp.broadcast_to(jnp.sum(jnp.where(same, row, 0.0), axis=1, keepdims=True), (n, width))


def depth_matrix(opacity, points):
    absorbers = opacity.shape[0]
    width = 4 * absorbers * LEVELS
    column = lax.broadcasted_iota(jnp.int32, (points, width), 1)
    held = jnp.zeros((points, width), F32)
    for a in range(absorbers):
        value = as_column(opacity[a : a + 1, :] * -LOG2E, width)
        for n, part in enumerate(parts_of(value, 2)):
            for m in range(2):
                held = jnp.where(column // LEVELS == (2 * n + m) * absorbers + a, part.astype(F32), held)
    level = lax.rem(column, LEVELS)
    return jnp.concatenate([jnp.where(level == i, held, 0.0) for i in range(LEVELS)], axis=0).astype(BF)


def sweep(depths, xs, t4, frac, lost, gain, levels, cells):
    points = frac.shape[0]
    halves = gain.shape[0]

    def fold(value):
        return jnp.sum(value.reshape(points // 8, 8, cells), axis=0)

    flux = jnp.zeros((points, cells), F32)
    for b in range(up_to(levels, LEVELS) // LEVELS):
        take = 1.0 - jnp.exp2(dot(depths, xs[b], NN))
        for i in range(min(LEVELS, levels - b * LEVELS)):
            l = b * LEVELS + i
            own = take[i * points : (i + 1) * points]
            lost[l] = own
            step = own * (frac * t4[l : l + 1, :] - flux)
            part = fold(step)
            for h in range(halves):
                gain[h, 8 * l : 8 * l + 8, :] = part[:, h * LANES : (h + 1) * LANES]
            flux = flux + step
    flux = 0.95 * (frac * t4[levels - 1 : levels, :]) + 0.05 * flux
    for l in range(levels - 1, -1, -1):
        step = lost[l] * (frac * t4[l : l + 1, :] - flux)
        part = fold(step)
        for h in range(halves):
            gain[h, 8 * l : 8 * l + 8, :] += part[:, h * LANES : (h + 1) * LANES]
        flux = flux + step


def radiate_kernel(plan, back, devices, levels, cells, arrived, opacity_in, fraction_in, out, opacity, fraction, sems, parts, match, mean, xs, t4, heat, lost, gain):
    copies = [
        pltpu.make_async_copy(opacity_in, opacity, sems.at[0]),
        pltpu.make_async_copy(fraction_in, fraction, sems.at[1]),
    ]
    for copy in copies:
        copy.start()
    fields = plan.fields
    lane = plan.rest
    slots = devices * CAP
    absorbers, points = opacity.shape
    tails = [arrived[pl.ds(CAP * plan.whole + j, devices, stride=plan.rows), :] for j in range(plan.tail)]
    pick = mask_to(lax.broadcasted_iota(jnp.int32, (8, LANES), 1) == lane - 1)
    rows = []
    for s in range(CAP):
        for k in range(plan.whole + 1):
            if k < plan.whole:
                value = arrived[pl.ds(CAP * k + s, devices, stride=plan.rows), :]
            else:
                value = plan.unpack(tails, s)
            split = parts_of(value, 2)
            for n, part in enumerate(split):
                first = n * slots + s * devices
                parts[first : first + devices, k * LANES : (k + 1) * LANES] = part
        cell = value[:, lane - 1 : lane].astype(jnp.int32)
        here = mask_to(cell == lax.broadcasted_iota(jnp.int32, (devices, cells), 1))
        for n in range(2):
            match[s * devices : (s + 1) * devices, n * cells : (n + 1) * cells] = here
        rows.append(dot(pick, split[0], NT)[0:1])
    cell_row = jnp.concatenate(rows, axis=1).astype(jnp.int32)
    turned = mask_to(lax.broadcasted_iota(jnp.int32, (cells, slots), 0) == cell_row)
    sums = jnp.transpose(dot(jnp.concatenate([turned, turned], axis=1), parts[...], NN))
    inverse = 1.0 / jnp.maximum(sums[fields - 2 : fields - 1, :], 1.0)
    warm = sums[0:levels] * inverse
    square = warm * warm
    t4[0:levels, :] = square * square
    block = mean.shape[0]
    mean[levels:, :] = jnp.zeros((block - levels, cells), F32)
    for a in range(absorbers):
        mean[0:levels, :] = sums[(a + 1) * levels : (a + 2) * levels] * inverse
        for n, part in enumerate(parts_of(mean[...], 2)):
            for m in range(2):
                first = ((2 * m + n) * absorbers + a) * LEVELS
                for b in range(block // LEVELS):
                    xs[b, first : first + LEVELS, :] = part[b * LEVELS : (b + 1) * LEVELS]
    for copy in copies:
        copy.wait()
    frac = as_column(fraction[...], cells)
    sweep(depth_matrix(opacity, points), xs, t4, frac, lost, gain, levels, cells)
    heat[...] = jnp.zeros(heat.shape, BF)
    for h in range(gain.shape[0]):
        total = gain[h, pl.ds(0, levels, stride=8), :]
        for g in range(1, 8):
            total = total + gain[h, pl.ds(g, levels, stride=8), :]
        for n, part in enumerate(parts_of(-total, 2)):
            first = n * cells + h * LANES
            heat[0:levels, first : first + LANES] = part
    acc = dot(match[...], heat[...], NT)
    for s in range(CAP):
        out[pl.ds(s, devices, stride=back.rows), :] = acc[s * devices : (s + 1) * devices, :LANES]
    rests = [acc[s * devices : (s + 1) * devices, LANES:] for s in range(CAP)]
    for j, tile in enumerate(back.pack(rests)):
        out[pl.ds(CAP + j, devices, stride=back.rows), :] = tile


def spread_kernel(back, devices, levels, chunks, returned, ones, slot, out, wide, held, sems):
    rows, columns = held.shape
    pieces = slot.shape[1]
    block = up_to(levels, 16)
    tails = [returned[pl.ds(CAP + j, devices, stride=back.rows), :] for j in range(back.tail)]
    for s in range(CAP):
        own = slice(s * devices, (s + 1) * devices)
        wide[own, :LANES] = returned[pl.ds(s, devices, stride=back.rows), :]
        wide[own, LANES:] = back.unpack(tails, s)
    turned = jnp.transpose(wide[...])[:block]
    both = dot(jnp.concatenate(parts_of(turned, 2), axis=0), slot[...], NN)
    both = jnp.concatenate(parts_of(both[:block] + both[block:], 2), axis=0)
    size = columns // chunks
    copies = []
    for c in range(chunks):
        own = slice(c * size, (c + 1) * size)
        value = dot(both, ones[:, own], NN)
        held[:, own] = value[:rows] + value[block : block + rows]
        copies.append(pltpu.make_async_copy(held.at[:, own], out.at[:, own], sems.at[c]))
        copies[-1].start()
    for copy in copies:
        copy.wait()


VMEM = pl.BlockSpec(memory_space=pltpu.VMEM)
HBM = pl.BlockSpec(memory_space=pl.ANY)


def params(mib):
    return pltpu.CompilerParams(vmem_limit_bytes=mib * MIB)


def in_hbm(value):
    return pltpu.with_memory_space_constraint(value, pltpu.HBM)


def plans(levels, species):
    fields = species * levels + 2
    return Plan(fields, up_to(fields % LANES, 16)), Plan(levels, up_to(levels % LANES, 16))


def gather_call(thermal, gas, weight_row, segment_row, target_row, box_row):
    levels, columns = thermal.shape
    species = gas.shape[1] + 1
    pieces = target_row.shape[1]
    devices = lax.axis_size(AXES)
    plan, _ = plans(levels, species)
    padded = (plan.whole + 1) * LANES
    slots = devices * CAP
    return pl.pallas_call(
        functools.partial(gather_kernel, plan, devices, (2, 2, 1)),
        out_shape=(
            jax.ShapeDtypeStruct((devices * plan.rows, LANES), F32),
            jax.ShapeDtypeStruct((pieces, columns), BF),
            jax.ShapeDtypeStruct((slots, pieces), BF),
        ),
        in_specs=[HBM] * 6,
        out_specs=(VMEM, VMEM, VMEM),
        scratch_shapes=[
            pltpu.VMEM((species, levels, columns), F32),
            pltpu.SemaphoreType.DMA((species + 4,)),
            pltpu.VMEM((1, columns), F32),
            pltpu.VMEM((1, columns), jnp.int32),
            pltpu.VMEM((1, pieces), jnp.int32),
            pltpu.VMEM((1, pieces), jnp.int32),
            pltpu.VMEM((2 * species * up_to(levels, 16) + 16, columns), BF),
            pltpu.VMEM((padded, 2 * pieces), BF),
        ],
        compiler_params=params(34),
        name="gather_pieces",
    )(*map(in_hbm, (thermal, gas, weight_row, segment_row, target_row, box_row)))


def radiate_call(arrived, opacity, fraction, levels, cells):
    absorbers, points = opacity.shape
    species = absorbers + 1
    devices = lax.axis_size(AXES)
    plan, back = plans(levels, species)
    padded = (plan.whole + 1) * LANES
    slots = devices * CAP
    block = up_to(levels, LEVELS)
    return pl.pallas_call(
        functools.partial(radiate_kernel, plan, back, devices, levels, cells),
        out_shape=jax.ShapeDtypeStruct((devices * back.rows, LANES), F32),
        in_specs=[VMEM, HBM, HBM],
        out_specs=VMEM,
        scratch_shapes=[
            pltpu.VMEM((absorbers, points), F32),
            pltpu.VMEM((1, points), F32),
            pltpu.SemaphoreType.DMA((2,)),
            pltpu.VMEM((2 * slots, padded), BF),
            pltpu.VMEM((slots, 2 * cells), BF),
            pltpu.VMEM((block, cells), F32),
            pltpu.VMEM((block // LEVELS, 4 * absorbers * LEVELS, cells), BF),
            pltpu.VMEM((block, cells), F32),
            pltpu.VMEM((2 * LANES, 2 * cells), BF),
            pltpu.VMEM((levels, points, cells), F32),
            pltpu.VMEM((cells // LANES, 8 * levels, LANES), F32),
        ],
        compiler_params=params(28),
        name="radiate_cells",
    )(arrived, in_hbm(opacity), in_hbm(fraction))


def spread_call(returned, ones, slot, levels):
    pieces, columns = ones.shape
    slots = slot.shape[0]
    devices = slots // CAP
    _, back = plans(levels, 1)
    chunks = 4
    return pl.pallas_call(
        functools.partial(spread_kernel, back, devices, levels, chunks),
        out_shape=jax.ShapeDtypeStruct((levels, columns), F32),
        in_specs=[VMEM, VMEM, VMEM],
        out_specs=HBM,
        scratch_shapes=[
            pltpu.VMEM((slots, 2 * LANES), F32),
            pltpu.VMEM((levels, columns), F32),
            pltpu.SemaphoreType.DMA((chunks,)),
        ],
        compiler_params=params(16),
        name="spread_heat",
    )(returned, ones, slot)


def exchange(value):
    devices = lax.axis_size(AXES)
    chunks = value.reshape(devices, 1, value.size // devices)
    return lax.all_to_all(chunks, AXES, split_axis=0, concat_axis=0, tiled=True).reshape(value.shape)


def shards(thermal, gas, footprint, segment, holder, box, opacity, fraction):
    levels, columns = thermal.shape
    pieces = box.shape[0]
    outgoing, ones, slot = gather_call(
        thermal,
        gas.transpose(1, 0, 2),
        footprint.reshape(1, columns),
        segment.reshape(1, columns),
        holder.reshape(1, pieces),
        box.reshape(1, pieces),
    )
    arrived = exchange(outgoing)
    heat = radiate_call(arrived, opacity.T, fraction.reshape(1, -1), levels, columns // 8)
    returned = exchange(heat)
    return spread_call(returned, ones, slot, levels)


def solution(mesh):
    placed = (
        P(None, AXES),
        P(None, None, AXES),
        P(AXES),
        P(AXES),
        P(AXES, None),
        P(AXES),
        P(),
        P(),
    )
    return jax.shard_map(shards, mesh=mesh, in_specs=placed, out_specs=P(None, AXES), check_vma=False)
```

```python
import functools

import jax
import jax.numpy as jnp
from jax import lax
from jax.experimental import pallas as pl
from jax.experimental.pallas import tpu as pltpu
from jax.sharding import PartitionSpec as P

AXES = ("dyn", "rad")
CAP = 8
LANES = 128
BF = jnp.bfloat16
F32 = jnp.float32
NT = (((1,), (1,)), ((), ()))
NN = (((1,), (0,)), ((), ()))
MIB = 1024 * 1024
FIRST = 2
LEVELS = 16
LOG2E = 1.4426950408889634


def up_to(value, step):
    return -(-value // step) * step


def parts_of(value, count):
    out = []
    for _ in range(count - 1):
        part = value.astype(BF)
        out.append(part)
        value = value - part.astype(F32)
    out.append(value.astype(BF))
    return out


def mask_to(mask):
    return jnp.where(mask, 1.0, 0.0).astype(BF)


def dot(a, b, dims):
    return lax.dot_general(a, b, dims, preferred_element_type=F32)


def slots_of(target, devices):
    pieces = target.shape[1]
    column = jnp.transpose(jnp.broadcast_to(target, (LANES, pieces)))
    ranks = []
    for j in range(pieces // LANES):
        part = target[:, j * LANES : (j + 1) * LANES]
        before = lax.broadcasted_iota(jnp.int32, (pieces, LANES), 0)
        me = lax.broadcasted_iota(jnp.int32, (pieces, LANES), 1) + j * LANES
        hit = (column == part) & (before < me)
        ranks.append(jnp.sum(jnp.where(hit, 1, 0), axis=0, keepdims=True))
    return jnp.concatenate(ranks, axis=1)


def slot_rows(target, rank, devices, store):
    pieces = target.shape[1]
    owner = lax.broadcasted_iota(jnp.int32, (devices, pieces), 0) == target
    for s in range(CAP):
        store(s, mask_to(owner & (rank == s)))


class Plan:
    def __init__(self, fields, width):
        self.fields = fields
        self.whole = fields // LANES
        self.rest = fields - self.whole * LANES
        self.width = width
        self.tail = up_to(CAP * width, LANES) // LANES
        self.rows = CAP * self.whole + self.tail

    def spans(self, s):
        start = s * self.width
        first, shift = start // LANES, start % LANES
        yield first, shift, None if shift + self.width <= LANES else "low"
        if shift + self.width > LANES:
            yield first + 1, shift, "high"

    def pack(self, rests):
        lane = lax.broadcasted_iota(jnp.int32, rests[0].shape, 1)
        tiles = [None] * self.tail
        for s, rest in enumerate(rests):
            for tile, shift, side in self.spans(s):
                part = pltpu.roll(rest, shift, 1) if shift else rest
                if side == "low":
                    part = jnp.where(lane >= shift, part, 0.0)
                if side == "high":
                    part = jnp.where(lane < shift, part, 0.0)
                tiles[tile] = part if tiles[tile] is None else tiles[tile] + part
        return tiles

    def unpack(self, tiles, s):
        spans = list(self.spans(s))
        value, shift = tiles[spans[0][0]], spans[0][1]
        if len(spans) == 2:
            lane = lax.broadcasted_iota(jnp.int32, value.shape, 1)
            value = jnp.where(lane >= shift, value, tiles[spans[1][0]])
        return pltpu.roll(value, LANES - shift, 1) if shift else value


def gather_kernel(plan, devices, groups, late, thermal, gas, weight_in, segment_in, target_in, box_in, out, ones, slot, buf, sems, weight, segment, target, box, left, comp):
    species, levels, columns = buf.shape
    pieces = target.shape[1]
    block = up_to(levels, 16)
    small = [(segment_in, segment), (weight_in, weight), (target_in, target), (box_in, box)]
    rows = [pltpu.make_async_copy(a, b, sems.at[species + n]) for n, (a, b) in enumerate(small)]
    for copy in rows:
        copy.start()
    copies = [pltpu.make_async_copy(thermal, buf.at[0], sems.at[0])]
    copies += [pltpu.make_async_copy(gas.at[:, k, :], buf.at[k + 1], sems.at[k + 1]) for k in range(species - 1)]
    for copy in copies[:FIRST]:
        copy.start()
    for copy in rows:
        copy.wait()
    for copy in copies[FIRST:]:
        copy.start()
    down = jnp.transpose(jnp.broadcast_to(segment[...], (LANES, columns)))
    for k in range(pieces // LANES):
        lane = lax.broadcasted_iota(jnp.int32, (columns, LANES), 1) + k * LANES
        ones[:, k * LANES : (k + 1) * LANES] = mask_to(down == lane)
    w = weight[...]
    end = 2 * species * block
    pair = parts_of(jnp.broadcast_to(w, (8, columns)), 2)
    left[end:, :] = jnp.concatenate([part.astype(F32) for part in pair], axis=0).astype(BF)

    def place():
        owner = target[...]
        rank = slots_of(owner, devices)

        def store(s, value):
            slot[s * devices : (s + 1) * devices, :] = value

        slot_rows(owner, rank, devices, store)

    def load(k):
        copies[k].wait()
        for n, part in enumerate(parts_of(buf[k] * w, 2)):
            left[(2 * k + n) * block : (2 * k + n) * block + levels, :] = part

    even = levels // 8 * 8
    spare = species * even

    def keep(k, sums, a):
        pair = sums[a : a + levels] + sums[a + block : a + block + levels]
        comp[k * even : (k + 1) * even, :] = pair[:even]
        return pair[even:]

    wide = 2 * LANES

    def emit(k):
        pair = parts_of(comp[k * wide : (k + 1) * wide, :], 2)
        acc = dot(slot[...], pair[0], NT) + dot(slot[...], pair[1], NT)
        for h in range(2):
            tile = 2 * k + h
            values = [acc[s * devices : (s + 1) * devices, h * LANES : (h + 1) * LANES] for s in range(CAP)]
            if tile < plan.whole:
                for s in range(CAP):
                    out[pl.ds(CAP * tile + s, devices, stride=plan.rows), :] = values[s]
            else:
                for j, value in enumerate(plan.pack(values)):
                    out[pl.ds(CAP * tile + j, devices, stride=plan.rows), :] = value

    emitted = 0
    ends = []
    bounds = [sum(groups[:n]) for n in range(len(groups) + 1)]
    for begin, stop in zip(bounds, bounds[1:]):
        last = stop == species
        for k in range(begin, stop):
            load(k)
        if begin == 0:
            place()
        sums = dot(left[2 * begin * block : end + 16 if last else 2 * stop * block, :], ones[...], NN)
        for k in range(begin, stop):
            a = 2 * (k - begin) * block
            ends.append(keep(k, sums, a))
        if last:
            a = 2 * (stop - begin) * block
            ends.append(sums[a : a + 1] + sums[a + 8 : a + 9])
            ends.append(box[...].astype(F32))
            row = lax.broadcasted_iota(jnp.int32, (comp.shape[0] - spare, pieces), 0)
            rest = jnp.zeros(row.shape, F32)
            for n, value in enumerate(ends):
                rest = jnp.where(row == n, value, rest)
            comp[spare:, :] = rest
        ready = comp.shape[0] if last or late else stop * even
        while (emitted + 1) * wide <= ready and (last or not late):
            emit(emitted)
            emitted += 1


def as_column(row, width):
    n = row.shape[1]
    same = lax.broadcasted_iota(jnp.int32, (n, n), 0) == lax.broadcasted_iota(jnp.int32, (n, n), 1)
    return jnp.broadcast_to(jnp.sum(jnp.where(same, row, 0.0), axis=1, keepdims=True), (n, width))


def depth_matrix(opacity, points):
    absorbers = opacity.shape[0]
    width = 4 * absorbers * LEVELS
    column = lax.broadcasted_iota(jnp.int32, (points, width), 1)
    held = jnp.zeros((points, width), F32)
    for a in range(absorbers):
        value = as_column(opacity[a : a + 1, :] * -LOG2E, width)
        for n, part in enumerate(parts_of(value, 2)):
            for m in range(2):
                held = jnp.where(column // LEVELS == (2 * n + m) * absorbers + a, part.astype(F32), held)
    level = lax.rem(column, LEVELS)
    return jnp.concatenate([jnp.where(level == i, held, 0.0) for i in range(LEVELS)], axis=0).astype(BF)


def sweep(depths, xs, t4, frac, lost, gain, levels, cells):
    points = frac.shape[0]
    halves = gain.shape[0]

    def fold(value):
        return jnp.sum(value.reshape(points // 8, 8, cells), axis=0)

    flux = jnp.zeros((points, cells), F32)
    for b in range(up_to(levels, LEVELS) // LEVELS):
        take = 1.0 - jnp.exp2(dot(depths, xs[b], NN))
        for i in range(min(LEVELS, levels - b * LEVELS)):
            l = b * LEVELS + i
            own = take[i * points : (i + 1) * points]
            lost[l] = own
            step = own * (frac * t4[l : l + 1, :] - flux)
            part = fold(step)
            for h in range(halves):
                gain[h, 8 * l : 8 * l + 8, :] = part[:, h * LANES : (h + 1) * LANES]
            flux = flux + step
    flux = 0.95 * (frac * t4[levels - 1 : levels, :]) + 0.05 * flux
    for l in range(levels - 1, -1, -1):
        step = lost[l] * (frac * t4[l : l + 1, :] - flux)
        part = fold(step)
        for h in range(halves):
            gain[h, 8 * l : 8 * l + 8, :] += part[:, h * LANES : (h + 1) * LANES]
        flux = flux + step


def radiate_kernel(plan, back, devices, levels, cells, arrived, opacity_in, fraction_in, out, opacity, fraction, sems, parts, match, mean, xs, t4, heat, lost, gain):
    copies = [
        pltpu.make_async_copy(opacity_in, opacity, sems.at[0]),
        pltpu.make_async_copy(fraction_in, fraction, sems.at[1]),
    ]
    for copy in copies:
        copy.start()
    fields = plan.fields
    lane = plan.rest
    slots = devices * CAP
    absorbers, points = opacity.shape
    tails = [arrived[pl.ds(CAP * plan.whole + j, devices, stride=plan.rows), :] for j in range(plan.tail)]
    pick = mask_to(lax.broadcasted_iota(jnp.int32, (8, LANES), 1) == lane - 1)
    rows = []
    for s in range(CAP):
        for k in range(plan.whole + 1):
            if k < plan.whole:
                value = arrived[pl.ds(CAP * k + s, devices, stride=plan.rows), :]
            else:
                value = plan.unpack(tails, s)
            split = parts_of(value, 2)
            for n, part in enumerate(split):
                first = n * slots + s * devices
                parts[first : first + devices, k * LANES : (k + 1) * LANES] = part
        cell = value[:, lane - 1 : lane].astype(jnp.int32)
        here = mask_to(cell == lax.broadcasted_iota(jnp.int32, (devices, cells), 1))
        for n in range(2):
            match[s * devices : (s + 1) * devices, n * cells : (n + 1) * cells] = here
        rows.append(dot(pick, split[0], NT)[0:1])
    cell_row = jnp.concatenate(rows, axis=1).astype(jnp.int32)
    turned = mask_to(lax.broadcasted_iota(jnp.int32, (cells, slots), 0) == cell_row)
    sums = jnp.transpose(dot(jnp.concatenate([turned, turned], axis=1), parts[...], NN))
    inverse = 1.0 / jnp.maximum(sums[fields - 2 : fields - 1, :], 1.0)
    even = levels // 8 * 8
    block = mean.shape[0]
    spare = (absorbers + 1) * even

    def means(k):
        row = lax.broadcasted_iota(jnp.int32, (block - even, cells), 0)
        mean[0:even, :] = sums[k * even : (k + 1) * even] * inverse
        mean[even:, :] = jnp.where(row == 0, sums[spare + k : spare + k + 1] * inverse, 0.0)
        return mean[...]

    warm = means(0)
    square = warm * warm
    t4[...] = square * square
    for a in range(absorbers):
        for n, part in enumerate(parts_of(means(a + 1), 2)):
            for m in range(2):
                first = ((2 * m + n) * absorbers + a) * LEVELS
                for b in range(block // LEVELS):
                    xs[b, first : first + LEVELS, :] = part[b * LEVELS : (b + 1) * LEVELS]
    for copy in copies:
        copy.wait()
    frac = as_column(fraction[...], cells)
    sweep(depth_matrix(opacity, points), xs, t4, frac, lost, gain, levels, cells)
    heat[...] = jnp.zeros(heat.shape, BF)
    for h in range(gain.shape[0]):
        total = gain[h, pl.ds(0, levels, stride=8), :]
        for g in range(1, 8):
            total = total + gain[h, pl.ds(g, levels, stride=8), :]
        for n, part in enumerate(parts_of(-total, 2)):
            first = n * cells + h * LANES
            heat[0:levels, first : first + LANES] = part
    acc = dot(match[...], heat[...], NT)
    for s in range(CAP):
        out[pl.ds(s, devices, stride=back.rows), :] = acc[s * devices : (s + 1) * devices, :LANES]
    rests = [acc[s * devices : (s + 1) * devices, LANES:] for s in range(CAP)]
    for j, tile in enumerate(back.pack(rests)):
        out[pl.ds(CAP + j, devices, stride=back.rows), :] = tile


def spread_kernel(back, devices, levels, chunks, returned, ones, slot, out, wide, held, sems):
    rows, columns = held.shape
    pieces = slot.shape[1]
    block = up_to(levels, 16)
    tails = [returned[pl.ds(CAP + j, devices, stride=back.rows), :] for j in range(back.tail)]
    for s in range(CAP):
        own = slice(s * devices, (s + 1) * devices)
        wide[own, :LANES] = returned[pl.ds(s, devices, stride=back.rows), :]
        wide[own, LANES:] = back.unpack(tails, s)
    turned = jnp.transpose(wide[...])[:block]
    both = dot(jnp.concatenate(parts_of(turned, 2), axis=0), slot[...], NN)
    both = jnp.concatenate(parts_of(both[:block] + both[block:], 2), axis=0)
    size = columns // chunks
    copies = []
    for c in range(chunks):
        own = slice(c * size, (c + 1) * size)
        value = dot(both, ones[own, :], NT)
        held[:, own] = value[:rows] + value[block : block + rows]
        copies.append(pltpu.make_async_copy(held.at[:, own], out.at[:, own], sems.at[c]))
        copies[-1].start()
    for copy in copies:
        copy.wait()


VMEM = pl.BlockSpec(memory_space=pltpu.VMEM)
HBM = pl.BlockSpec(memory_space=pl.ANY)


def params(mib):
    return pltpu.CompilerParams(vmem_limit_bytes=mib * MIB)


def in_hbm(value):
    return pltpu.with_memory_space_constraint(value, pltpu.HBM)


def plans(levels, species):
    fields = species * levels + 2
    return Plan(fields, up_to(fields % LANES, 16)), Plan(levels, up_to(levels % LANES, 16))


def gather_call(thermal, gas, weight_row, segment_row, target_row, box_row):
    levels, columns = thermal.shape
    species = gas.shape[1] + 1
    pieces = target_row.shape[1]
    devices = lax.axis_size(AXES)
    plan, _ = plans(levels, species)
    padded = (plan.whole + 1) * LANES
    slots = devices * CAP
    return pl.pallas_call(
        functools.partial(gather_kernel, plan, devices, (1, 1, 1, 1, 1), True),
        out_shape=(
            jax.ShapeDtypeStruct((devices * plan.rows, LANES), F32),
            jax.ShapeDtypeStruct((columns, pieces), BF),
            jax.ShapeDtypeStruct((slots, pieces), BF),
        ),
        in_specs=[HBM] * 6,
        out_specs=(VMEM, VMEM, VMEM),
        scratch_shapes=[
            pltpu.VMEM((species, levels, columns), F32),
            pltpu.SemaphoreType.DMA((species + 4,)),
            pltpu.VMEM((1, columns), F32),
            pltpu.VMEM((1, columns), jnp.int32),
            pltpu.VMEM((1, pieces), jnp.int32),
            pltpu.VMEM((1, pieces), jnp.int32),
            pltpu.VMEM((2 * species * up_to(levels, 16) + 16, columns), BF),
            pltpu.VMEM((padded, pieces), F32),
        ],
        compiler_params=params(34),
        name="gather_pieces",
    )(*map(in_hbm, (thermal, gas, weight_row, segment_row, target_row, box_row)))


def radiate_call(arrived, opacity, fraction, levels, cells):
    absorbers, points = opacity.shape
    species = absorbers + 1
    devices = lax.axis_size(AXES)
    plan, back = plans(levels, species)
    padded = (plan.whole + 1) * LANES
    slots = devices * CAP
    block = up_to(levels, LEVELS)
    return pl.pallas_call(
        functools.partial(radiate_kernel, plan, back, devices, levels, cells),
        out_shape=jax.ShapeDtypeStruct((devices * back.rows, LANES), F32),
        in_specs=[VMEM, HBM, HBM],
        out_specs=VMEM,
        scratch_shapes=[
            pltpu.VMEM((absorbers, points), F32),
            pltpu.VMEM((1, points), F32),
            pltpu.SemaphoreType.DMA((2,)),
            pltpu.VMEM((2 * slots, padded), BF),
            pltpu.VMEM((slots, 2 * cells), BF),
            pltpu.VMEM((block, cells), F32),
            pltpu.VMEM((block // LEVELS, 4 * absorbers * LEVELS, cells), BF),
            pltpu.VMEM((block, cells), F32),
            pltpu.VMEM((2 * LANES, 2 * cells), BF),
            pltpu.VMEM((levels, points, cells), F32),
            pltpu.VMEM((cells // LANES, 8 * levels, LANES), F32),
        ],
        compiler_params=params(28),
        name="radiate_cells",
    )(arrived, in_hbm(opacity), in_hbm(fraction))


def spread_call(returned, ones, slot, levels):
    columns, pieces = ones.shape
    slots = slot.shape[0]
    devices = slots // CAP
    _, back = plans(levels, 1)
    chunks = 4
    return pl.pallas_call(
        functools.partial(spread_kernel, back, devices, levels, chunks),
        out_shape=jax.ShapeDtypeStruct((levels, columns), F32),
        in_specs=[VMEM, VMEM, VMEM],
        out_specs=HBM,
        scratch_shapes=[
            pltpu.VMEM((slots, 2 * LANES), F32),
            pltpu.VMEM((levels, columns), F32),
            pltpu.SemaphoreType.DMA((chunks,)),
        ],
        compiler_params=params(16),
        name="spread_heat",
    )(returned, ones, slot)


def exchange(value):
    devices = lax.axis_size(AXES)
    chunks = value.reshape(devices, 1, value.size // devices)
    return lax.all_to_all(chunks, AXES, split_axis=0, concat_axis=0, tiled=True).reshape(value.shape)


def shards(thermal, gas, footprint, segment, holder, box, opacity, fraction):
    levels, columns = thermal.shape
    pieces = box.shape[0]
    outgoing, ones, slot = gather_call(
        thermal,
        gas.transpose(1, 0, 2),
        footprint.reshape(1, columns),
        segment.reshape(1, columns),
        holder.reshape(1, pieces),
        box.reshape(1, pieces),
    )
    arrived = exchange(outgoing)
    heat = radiate_call(arrived, opacity.T, fraction.reshape(1, -1), levels, columns // 8)
    returned = exchange(heat)
    return spread_call(returned, ones, slot, levels)


def solution(mesh):
    placed = (
        P(None, AXES),
        P(None, None, AXES),
        P(AXES),
        P(AXES),
        P(AXES, None),
        P(AXES),
        P(),
        P(),
    )
    return jax.shard_map(shards, mesh=mesh, in_specs=placed, out_specs=P(None, AXES), check_vma=False)
```

```python
import functools

import jax
import jax.numpy as jnp
from jax import lax
from jax.experimental import pallas as pl
from jax.experimental.pallas import tpu as pltpu
from jax.sharding import PartitionSpec as P

AXES = ("dyn", "rad")
CAP = 8
LANES = 128
BF = jnp.bfloat16
F32 = jnp.float32
NT = (((1,), (1,)), ((), ()))
NN = (((1,), (0,)), ((), ()))
MIB = 1024 * 1024
FIRST = 2
BATCHES = {0: 2, 2: 5}
LEVELS = 16
LOG2E = 1.4426950408889634


def up_to(value, step):
    return -(-value // step) * step


def parts_of(value, count):
    out = []
    for _ in range(count - 1):
        part = value.astype(BF)
        out.append(part)
        value = value - part.astype(F32)
    out.append(value.astype(BF))
    return out


def mask_to(mask):
    return jnp.where(mask, 1.0, 0.0).astype(BF)


def dot(a, b, dims):
    return lax.dot_general(a, b, dims, preferred_element_type=F32)


def slots_of(target, devices):
    pieces = target.shape[1]
    column = jnp.transpose(jnp.broadcast_to(target, (LANES, pieces)))
    ranks = []
    for j in range(pieces // LANES):
        part = target[:, j * LANES : (j + 1) * LANES]
        before = lax.broadcasted_iota(jnp.int32, (pieces, LANES), 0)
        me = lax.broadcasted_iota(jnp.int32, (pieces, LANES), 1) + j * LANES
        hit = (column == part) & (before < me)
        ranks.append(jnp.sum(jnp.where(hit, 1, 0), axis=0, keepdims=True))
    return jnp.concatenate(ranks, axis=1)


def slot_rows(target, rank, devices, store):
    pieces = target.shape[1]
    owner = lax.broadcasted_iota(jnp.int32, (devices, pieces), 0) == target
    for s in range(CAP):
        store(s, mask_to(owner & (rank == s)))


class Plan:
    def __init__(self, fields, width):
        self.fields = fields
        self.whole = fields // LANES
        self.rest = fields - self.whole * LANES
        self.width = width
        self.tail = up_to(CAP * width, LANES) // LANES
        self.rows = CAP * self.whole + self.tail

    def spans(self, s):
        start = s * self.width
        first, shift = start // LANES, start % LANES
        yield first, shift, None if shift + self.width <= LANES else "low"
        if shift + self.width > LANES:
            yield first + 1, shift, "high"

    def pack(self, rests):
        lane = lax.broadcasted_iota(jnp.int32, rests[0].shape, 1)
        tiles = [None] * self.tail
        for s, rest in enumerate(rests):
            for tile, shift, side in self.spans(s):
                part = pltpu.roll(rest, shift, 1) if shift else rest
                if side == "low":
                    part = jnp.where(lane >= shift, part, 0.0)
                if side == "high":
                    part = jnp.where(lane < shift, part, 0.0)
                tiles[tile] = part if tiles[tile] is None else tiles[tile] + part
        return tiles

    def unpack(self, tiles, s):
        spans = list(self.spans(s))
        value, shift = tiles[spans[0][0]], spans[0][1]
        if len(spans) == 2:
            lane = lax.broadcasted_iota(jnp.int32, value.shape, 1)
            value = jnp.where(lane >= shift, value, tiles[spans[1][0]])
        return pltpu.roll(value, LANES - shift, 1) if shift else value


def gather_kernel(plan, devices, groups, late, thermal, gas, weight_in, segment_in, target_in, box_in, out, ones, slot, buf, sems, weight, segment, target, box, left, comp):
    species, levels, columns = buf.shape
    pieces = target.shape[1]
    block = up_to(levels, 16)
    small = [(segment_in, segment), (weight_in, weight), (target_in, target), (box_in, box)]
    rows = [pltpu.make_async_copy(a, b, sems.at[species + n]) for n, (a, b) in enumerate(small)]
    for copy in rows:
        copy.start()
    copies = [pltpu.make_async_copy(thermal, buf.at[0], sems.at[0])]
    copies += [pltpu.make_async_copy(gas.at[:, k, :], buf.at[k + 1], sems.at[k + 1]) for k in range(species - 1)]
    for copy in copies[:FIRST]:
        copy.start()
    for copy in rows:
        copy.wait()
    for copy in copies[FIRST:]:
        copy.start()
    down = jnp.transpose(jnp.broadcast_to(segment[...], (LANES, columns)))
    for k in range(pieces // LANES):
        lane = lax.broadcasted_iota(jnp.int32, (columns, LANES), 1) + k * LANES
        ones[:, k * LANES : (k + 1) * LANES] = mask_to(down == lane)
    w = weight[...]
    end = 2 * species * block
    pair = parts_of(jnp.broadcast_to(w, (8, columns)), 2)
    left[end:, :] = jnp.concatenate([part.astype(F32) for part in pair], axis=0).astype(BF)

    def place():
        owner = target[...]
        rank = slots_of(owner, devices)

        def store(s, value):
            slot[s * devices : (s + 1) * devices, :] = value

        slot_rows(owner, rank, devices, store)

    def load(k):
        if k in BATCHES:
            for copy in copies[k : BATCHES[k]]:
                copy.wait()
        for n, part in enumerate(parts_of(buf[k] * w, 2)):
            left[(2 * k + n) * block : (2 * k + n) * block + levels, :] = part

    even = levels // 8 * 8
    spare = species * even

    def keep(k, sums, a):
        pair = sums[a : a + levels] + sums[a + block : a + block + levels]
        comp[k * even : (k + 1) * even, :] = pair[:even]
        return pair[even:]

    wide = 2 * LANES

    def emit(k):
        pair = parts_of(comp[k * wide : (k + 1) * wide, :], 2)
        acc = dot(slot[...], pair[0], NT) + dot(slot[...], pair[1], NT)
        for h in range(2):
            tile = 2 * k + h
            values = [acc[s * devices : (s + 1) * devices, h * LANES : (h + 1) * LANES] for s in range(CAP)]
            if tile < plan.whole:
                for s in range(CAP):
                    out[pl.ds(CAP * tile + s, devices, stride=plan.rows), :] = values[s]
            else:
                for j, value in enumerate(plan.pack(values)):
                    out[pl.ds(CAP * tile + j, devices, stride=plan.rows), :] = value

    emitted = 0
    ends = []
    bounds = [sum(groups[:n]) for n in range(len(groups) + 1)]
    for begin, stop in zip(bounds, bounds[1:]):
        last = stop == species
        for k in range(begin, stop):
            load(k)
        if begin == 0:
            place()
        sums = dot(left[2 * begin * block : end + 16 if last else 2 * stop * block, :], ones[...], NN)
        for k in range(begin, stop):
            a = 2 * (k - begin) * block
            ends.append(keep(k, sums, a))
        if last:
            a = 2 * (stop - begin) * block
            ends.append(sums[a : a + 1] + sums[a + 8 : a + 9])
            ends.append(box[...].astype(F32))
            row = lax.broadcasted_iota(jnp.int32, (comp.shape[0] - spare, pieces), 0)
            rest = jnp.zeros(row.shape, F32)
            for n, value in enumerate(ends):
                rest = jnp.where(row == n, value, rest)
            comp[spare:, :] = rest
        ready = comp.shape[0] if last or late else stop * even
        while (emitted + 1) * wide <= ready and (last or not late):
            emit(emitted)
            emitted += 1


def as_column(row, width):
    n = row.shape[1]
    same = lax.broadcasted_iota(jnp.int32, (n, n), 0) == lax.broadcasted_iota(jnp.int32, (n, n), 1)
    return jnp.broadcast_to(jnp.sum(jnp.where(same, row, 0.0), axis=1, keepdims=True), (n, width))


def depth_matrix(opacity, points):
    absorbers = opacity.shape[0]
    width = 4 * absorbers * LEVELS
    column = lax.broadcasted_iota(jnp.int32, (points, width), 1)
    held = jnp.zeros((points, width), F32)
    for a in range(absorbers):
        value = as_column(opacity[a : a + 1, :] * -LOG2E, width)
        for n, part in enumerate(parts_of(value, 2)):
            for m in range(2):
                held = jnp.where(column // LEVELS == (2 * n + m) * absorbers + a, part.astype(F32), held)
    level = lax.rem(column, LEVELS)
    return jnp.concatenate([jnp.where(level == i, held, 0.0) for i in range(LEVELS)], axis=0).astype(BF)


def sweep(depths, xs, rise, first, frac, kept, below, above, levels, cells):
    points = frac.shape[0]
    halves = below.shape[0]

    def hold(ref, l, value):
        part = jnp.sum(value.reshape(points // 8, 8, cells), axis=0)
        for h in range(halves):
            ref[h, 8 * l : 8 * l + 8, :] = part[:, h * LANES : (h + 1) * LANES]

    lack = frac * first
    through = lack
    for b in range(up_to(levels, LEVELS) // LEVELS):
        trans = jnp.exp2(dot(depths, xs[b], NN))
        for i in range(min(LEVELS, levels - b * LEVELS)):
            l = b * LEVELS + i
            own = trans[i * points : (i + 1) * points]
            kept[l] = own
            through = own * lack
            hold(below, l, through)
            if l + 1 < levels:
                lack = through + frac * rise[l : l + 1, :]
    lack = 0.05 * through
    for l in range(levels - 1, -1, -1):
        through = kept[l] * lack
        hold(above, l, through)
        if l:
            lack = through - frac * rise[l - 1 : l, :]


def taken(below, above, rise, first, frac, enter, h, levels):
    lanes = slice(h * LANES, (h + 1) * LANES)

    def total(ref):
        value = ref[h, pl.ds(0, levels, stride=8), :]
        for g in range(1, 8):
            value = value + ref[h, pl.ds(g, levels, stride=8), :]
        return value

    down, up = total(below), total(above)
    weight = jnp.sum(frac[:, lanes], axis=0, keepdims=True)
    change = weight * rise[0 : levels - 1, lanes]
    enter[0:1, :] = weight * first[:, lanes]
    enter[1:levels, :] = down[: levels - 1] + change
    value = enter[0:levels, :] - down
    enter[0 : levels - 1, :] = up[1:] - change
    enter[levels - 1 : levels, :] = 0.05 * down[levels - 1 :]
    return value + (enter[0:levels, :] - up)


def radiate_kernel(plan, back, devices, levels, cells, arrived, opacity_in, fraction_in, out, opacity, fraction, sems, parts, match, mean, xs, t4, rise, heat, kept, below, above, enter):
    copies = [
        pltpu.make_async_copy(opacity_in, opacity, sems.at[0]),
        pltpu.make_async_copy(fraction_in, fraction, sems.at[1]),
    ]
    for copy in copies:
        copy.start()
    fields = plan.fields
    lane = plan.rest
    slots = devices * CAP
    absorbers, points = opacity.shape
    tails = [arrived[pl.ds(CAP * plan.whole + j, devices, stride=plan.rows), :] for j in range(plan.tail)]
    pick = mask_to(lax.broadcasted_iota(jnp.int32, (8, LANES), 1) == lane - 1)
    rows = []
    for s in range(CAP):
        for k in range(plan.whole + 1):
            if k < plan.whole:
                value = arrived[pl.ds(CAP * k + s, devices, stride=plan.rows), :]
            else:
                value = plan.unpack(tails, s)
            split = parts_of(value, 2)
            for n, part in enumerate(split):
                first = n * slots + s * devices
                parts[first : first + devices, k * LANES : (k + 1) * LANES] = part
        cell = value[:, lane - 1 : lane].astype(jnp.int32)
        here = mask_to(cell == lax.broadcasted_iota(jnp.int32, (devices, cells), 1))
        for n in range(2):
            match[s * devices : (s + 1) * devices, n * cells : (n + 1) * cells] = here
        rows.append(dot(pick, split[0], NT)[0:1])
    cell_row = jnp.concatenate(rows, axis=1).astype(jnp.int32)
    turned = mask_to(lax.broadcasted_iota(jnp.int32, (cells, slots), 0) == cell_row)
    sums = jnp.transpose(dot(jnp.concatenate([turned, turned], axis=1), parts[...], NN))
    inverse = 1.0 / jnp.maximum(sums[fields - 2 : fields - 1, :], 1.0)
    even = levels // 8 * 8
    block = mean.shape[0]
    spare = (absorbers + 1) * even

    def means(k):
        row = lax.broadcasted_iota(jnp.int32, (block - even, cells), 0)
        mean[0:even, :] = sums[k * even : (k + 1) * even] * inverse
        mean[even:, :] = jnp.where(row == 0, sums[spare + k : spare + k + 1] * inverse, 0.0)
        return mean[...]

    warm = means(0)
    square = warm * warm
    t4[...] = square * square
    rise[0 : levels - 1, :] = t4[1:levels, :] - t4[0 : levels - 1, :]
    for a in range(absorbers):
        for n, part in enumerate(parts_of(means(a + 1), 2)):
            for m in range(2):
                first = ((2 * m + n) * absorbers + a) * LEVELS
                for b in range(block // LEVELS):
                    xs[b, first : first + LEVELS, :] = part[b * LEVELS : (b + 1) * LEVELS]
    for copy in copies:
        copy.wait()
    frac = as_column(fraction[...], cells)
    top = t4[0:1, :]
    sweep(depth_matrix(opacity, points), xs, rise, top, frac, kept, below, above, levels, cells)
    heat[...] = jnp.zeros(heat.shape, BF)
    for h in range(below.shape[0]):
        total = taken(below, above, rise, top, frac, enter, h, levels)
        for n, part in enumerate(parts_of(-total, 2)):
            first = n * cells + h * LANES
            heat[0:levels, first : first + LANES] = part
    acc = dot(match[...], heat[...], NT)
    for s in range(CAP):
        out[pl.ds(s, devices, stride=back.rows), :] = acc[s * devices : (s + 1) * devices, :LANES]
    rests = [acc[s * devices : (s + 1) * devices, LANES:] for s in range(CAP)]
    for j, tile in enumerate(back.pack(rests)):
        out[pl.ds(CAP + j, devices, stride=back.rows), :] = tile


def spread_kernel(back, devices, levels, chunks, returned, ones, slot, out, wide, held, sems):
    rows, columns = held.shape
    pieces = slot.shape[1]
    block = up_to(levels, 16)
    tails = [returned[pl.ds(CAP + j, devices, stride=back.rows), :] for j in range(back.tail)]
    for s in range(CAP):
        own = slice(s * devices, (s + 1) * devices)
        wide[own, :LANES] = returned[pl.ds(s, devices, stride=back.rows), :]
        wide[own, LANES:] = back.unpack(tails, s)
    turned = jnp.transpose(wide[...])[:block]
    both = dot(jnp.concatenate(parts_of(turned, 2), axis=0), slot[...], NN)
    both = jnp.concatenate(parts_of(both[:block] + both[block:], 2), axis=0)
    size = columns // chunks
    copies = []
    for c in range(chunks):
        own = slice(c * size, (c + 1) * size)
        value = dot(both, ones[own, :], NT)
        held[:, own] = value[:rows] + value[block : block + rows]
        copies.append(pltpu.make_async_copy(held.at[:, own], out.at[:, own], sems.at[c]))
        copies[-1].start()
    for copy in copies:
        copy.wait()


VMEM = pl.BlockSpec(memory_space=pltpu.VMEM)
HBM = pl.BlockSpec(memory_space=pl.ANY)


def params(mib):
    return pltpu.CompilerParams(vmem_limit_bytes=mib * MIB)


def in_hbm(value):
    return pltpu.with_memory_space_constraint(value, pltpu.HBM)


def plans(levels, species):
    fields = species * levels + 2
    return Plan(fields, up_to(fields % LANES, 16)), Plan(levels, up_to(levels % LANES, 16))


def gather_call(thermal, gas, weight_row, segment_row, target_row, box_row):
    levels, columns = thermal.shape
    species = gas.shape[1] + 1
    pieces = target_row.shape[1]
    devices = lax.axis_size(AXES)
    plan, _ = plans(levels, species)
    padded = (plan.whole + 1) * LANES
    slots = devices * CAP
    return pl.pallas_call(
        functools.partial(gather_kernel, plan, devices, (2, 3), True),
        out_shape=(
            jax.ShapeDtypeStruct((devices * plan.rows, LANES), F32),
            jax.ShapeDtypeStruct((columns, pieces), BF),
            jax.ShapeDtypeStruct((slots, pieces), BF),
        ),
        in_specs=[HBM] * 6,
        out_specs=(VMEM, VMEM, VMEM),
        scratch_shapes=[
            pltpu.VMEM((species, levels, columns), F32),
            pltpu.SemaphoreType.DMA((species + 4,)),
            pltpu.VMEM((1, columns), F32),
            pltpu.VMEM((1, columns), jnp.int32),
            pltpu.VMEM((1, pieces), jnp.int32),
            pltpu.VMEM((1, pieces), jnp.int32),
            pltpu.VMEM((2 * species * up_to(levels, 16) + 16, columns), BF),
            pltpu.VMEM((padded, pieces), F32),
        ],
        compiler_params=params(34),
        name="gather_pieces",
    )(*map(in_hbm, (thermal, gas, weight_row, segment_row, target_row, box_row)))


def radiate_call(arrived, opacity, fraction, levels, cells):
    absorbers, points = opacity.shape
    species = absorbers + 1
    devices = lax.axis_size(AXES)
    plan, back = plans(levels, species)
    padded = (plan.whole + 1) * LANES
    slots = devices * CAP
    block = up_to(levels, LEVELS)
    return pl.pallas_call(
        functools.partial(radiate_kernel, plan, back, devices, levels, cells),
        out_shape=jax.ShapeDtypeStruct((devices * back.rows, LANES), F32),
        in_specs=[VMEM, HBM, HBM],
        out_specs=VMEM,
        scratch_shapes=[
            pltpu.VMEM((absorbers, points), F32),
            pltpu.VMEM((1, points), F32),
            pltpu.SemaphoreType.DMA((2,)),
            pltpu.VMEM((2 * slots, padded), BF),
            pltpu.VMEM((slots, 2 * cells), BF),
            pltpu.VMEM((block, cells), F32),
            pltpu.VMEM((block // LEVELS, 4 * absorbers * LEVELS, cells), BF),
            pltpu.VMEM((block, cells), F32),
            pltpu.VMEM((block, cells), F32),
            pltpu.VMEM((2 * LANES, 2 * cells), BF),
            pltpu.VMEM((levels, points, cells), F32),
            pltpu.VMEM((cells // LANES, 8 * levels, LANES), F32),
            pltpu.VMEM((cells // LANES, 8 * levels, LANES), F32),
            pltpu.VMEM((block, LANES), F32),
        ],
        compiler_params=params(28),
        name="radiate_cells",
    )(arrived, in_hbm(opacity), in_hbm(fraction))


def spread_call(returned, ones, slot, levels):
    columns, pieces = ones.shape
    slots = slot.shape[0]
    devices = slots // CAP
    _, back = plans(levels, 1)
    chunks = 4
    return pl.pallas_call(
        functools.partial(spread_kernel, back, devices, levels, chunks),
        out_shape=jax.ShapeDtypeStruct((levels, columns), F32),
        in_specs=[VMEM, VMEM, VMEM],
        out_specs=HBM,
        scratch_shapes=[
            pltpu.VMEM((slots, 2 * LANES), F32),
            pltpu.VMEM((levels, columns), F32),
            pltpu.SemaphoreType.DMA((chunks,)),
        ],
        compiler_params=params(16),
        name="spread_heat",
    )(returned, ones, slot)


def exchange(value):
    devices = lax.axis_size(AXES)
    chunks = value.reshape(devices, 1, value.size // devices)
    return lax.all_to_all(chunks, AXES, split_axis=0, concat_axis=0, tiled=True).reshape(value.shape)


def shards(thermal, gas, footprint, segment, holder, box, opacity, fraction):
    levels, columns = thermal.shape
    pieces = box.shape[0]
    outgoing, ones, slot = gather_call(
        thermal,
        gas.transpose(1, 0, 2),
        footprint.reshape(1, columns),
        segment.reshape(1, columns),
        holder.reshape(1, pieces),
        box.reshape(1, pieces),
    )
    arrived = exchange(outgoing)
    heat = radiate_call(arrived, opacity.T, fraction.reshape(1, -1), levels, columns // 8)
    returned = exchange(heat)
    return spread_call(returned, ones, slot, levels)


def solution(mesh):
    placed = (
        P(None, AXES),
        P(None, None, AXES),
        P(AXES),
        P(AXES),
        P(AXES, None),
        P(AXES),
        P(),
        P(),
    )
    return jax.shard_map(shards, mesh=mesh, in_specs=placed, out_specs=P(None, AXES), check_vma=False)
```

```python
import functools

import jax
import jax.numpy as jnp
from jax import lax
from jax.experimental import pallas as pl
from jax.experimental.pallas import tpu as pltpu
from jax.sharding import PartitionSpec as P

AXES = ("dyn", "rad")
CAP = 8
LANES = 128
BF = jnp.bfloat16
F32 = jnp.float32
NT = (((1,), (1,)), ((), ()))
NN = (((1,), (0,)), ((), ()))
MIB = 1024 * 1024
FIRST = 2
BATCHES = {0: 2, 2: 5}
LEVELS = 16
LOG2E = 1.4426950408889634


def up_to(value, step):
    return -(-value // step) * step


def parts_of(value, count):
    out = []
    for _ in range(count - 1):
        part = value.astype(BF)
        out.append(part)
        value = value - part.astype(F32)
    out.append(value.astype(BF))
    return out


def mask_to(mask):
    return jnp.where(mask, 1.0, 0.0).astype(BF)


def dot(a, b, dims):
    return lax.dot_general(a, b, dims, preferred_element_type=F32)


def slots_of(target, devices):
    pieces = target.shape[1]
    column = jnp.transpose(jnp.broadcast_to(target, (LANES, pieces)))
    ranks = []
    for j in range(pieces // LANES):
        part = target[:, j * LANES : (j + 1) * LANES]
        before = lax.broadcasted_iota(jnp.int32, (pieces, LANES), 0)
        me = lax.broadcasted_iota(jnp.int32, (pieces, LANES), 1) + j * LANES
        hit = (column == part) & (before < me)
        ranks.append(jnp.sum(jnp.where(hit, 1, 0), axis=0, keepdims=True))
    return jnp.concatenate(ranks, axis=1)


def slot_rows(target, rank, devices, store):
    pieces = target.shape[1]
    owner = lax.broadcasted_iota(jnp.int32, (devices, pieces), 0) == target
    for s in range(CAP):
        store(s, mask_to(owner & (rank == s)))


class Plan:
    def __init__(self, fields, width):
        self.fields = fields
        self.whole = fields // LANES
        self.rest = fields - self.whole * LANES
        self.width = width
        self.tail = up_to(CAP * width, LANES) // LANES
        self.rows = CAP * self.whole + self.tail

    def spans(self, s):
        start = s * self.width
        first, shift = start // LANES, start % LANES
        yield first, shift, None if shift + self.width <= LANES else "low"
        if shift + self.width > LANES:
            yield first + 1, shift, "high"

    def pack(self, rests):
        lane = lax.broadcasted_iota(jnp.int32, rests[0].shape, 1)
        tiles = [None] * self.tail
        for s, rest in enumerate(rests):
            for tile, shift, side in self.spans(s):
                part = pltpu.roll(rest, shift, 1) if shift else rest
                if side == "low":
                    part = jnp.where(lane >= shift, part, 0.0)
                if side == "high":
                    part = jnp.where(lane < shift, part, 0.0)
                tiles[tile] = part if tiles[tile] is None else tiles[tile] + part
        return tiles

    def unpack(self, tiles, s):
        spans = list(self.spans(s))
        value, shift = tiles[spans[0][0]], spans[0][1]
        if len(spans) == 2:
            lane = lax.broadcasted_iota(jnp.int32, value.shape, 1)
            value = jnp.where(lane >= shift, value, tiles[spans[1][0]])
        return pltpu.roll(value, LANES - shift, 1) if shift else value


def gather_kernel(plan, devices, groups, late, thermal, gas, weight_in, segment_in, target_in, box_in, out, ones, slot, buf, sems, weight, segment, target, box, left, comp):
    species, levels, columns = buf.shape
    pieces = target.shape[1]
    block = up_to(levels, 16)
    small = [(segment_in, segment), (weight_in, weight), (target_in, target), (box_in, box)]
    rows = [pltpu.make_async_copy(a, b, sems.at[species + n]) for n, (a, b) in enumerate(small)]
    for copy in rows:
        copy.start()
    copies = [pltpu.make_async_copy(thermal, buf.at[0], sems.at[0])]
    copies += [pltpu.make_async_copy(gas.at[:, k, :], buf.at[k + 1], sems.at[k + 1]) for k in range(species - 1)]
    for copy in copies[:FIRST]:
        copy.start()
    for copy in rows:
        copy.wait()
    for copy in copies[FIRST:]:
        copy.start()
    down = jnp.transpose(jnp.broadcast_to(segment[...], (LANES, columns)))
    for k in range(pieces // LANES):
        lane = lax.broadcasted_iota(jnp.int32, (columns, LANES), 1) + k * LANES
        ones[:, k * LANES : (k + 1) * LANES] = mask_to(down == lane)
    w = weight[...]
    end = 2 * species * block
    pair = parts_of(jnp.broadcast_to(w, (8, columns)), 2)
    left[end:, :] = jnp.concatenate([part.astype(F32) for part in pair], axis=0).astype(BF)

    def place():
        owner = target[...]
        rank = slots_of(owner, devices)

        def store(s, value):
            slot[s * devices : (s + 1) * devices, :] = value

        slot_rows(owner, rank, devices, store)

    def load(k):
        if k in BATCHES:
            for copy in copies[k : BATCHES[k]]:
                copy.wait()
        for n, part in enumerate(parts_of(buf[k] * w, 2)):
            left[(2 * k + n) * block : (2 * k + n) * block + levels, :] = part

    even = levels // 8 * 8
    spare = species * even

    def keep(k, sums, a):
        pair = sums[a : a + levels] + sums[a + block : a + block + levels]
        comp[k * even : (k + 1) * even, :] = pair[:even]
        return pair[even:]

    wide = 2 * LANES

    def emit(k):
        pair = parts_of(comp[k * wide : (k + 1) * wide, :], 2)
        acc = dot(slot[...], pair[0], NT) + dot(slot[...], pair[1], NT)
        for h in range(2):
            tile = 2 * k + h
            values = [acc[s * devices : (s + 1) * devices, h * LANES : (h + 1) * LANES] for s in range(CAP)]
            if tile < plan.whole:
                for s in range(CAP):
                    out[pl.ds(CAP * tile + s, devices, stride=plan.rows), :] = values[s]
            else:
                for j, value in enumerate(plan.pack(values)):
                    out[pl.ds(CAP * tile + j, devices, stride=plan.rows), :] = value

    emitted = 0
    ends = []
    bounds = [sum(groups[:n]) for n in range(len(groups) + 1)]
    for begin, stop in zip(bounds, bounds[1:]):
        last = stop == species
        for k in range(begin, stop):
            load(k)
        if begin == 0:
            place()
        sums = dot(left[2 * begin * block : end + 16 if last else 2 * stop * block, :], ones[...], NN)
        for k in range(begin, stop):
            a = 2 * (k - begin) * block
            ends.append(keep(k, sums, a))
        if last:
            a = 2 * (stop - begin) * block
            ends.append(sums[a : a + 1] + sums[a + 8 : a + 9])
            ends.append(box[...].astype(F32))
            row = lax.broadcasted_iota(jnp.int32, (comp.shape[0] - spare, pieces), 0)
            rest = jnp.zeros(row.shape, F32)
            for n, value in enumerate(ends):
                rest = jnp.where(row == n, value, rest)
            comp[spare:, :] = rest
        ready = comp.shape[0] if last or late else stop * even
        while (emitted + 1) * wide <= ready and (last or not late):
            emit(emitted)
            emitted += 1


def as_column(row, width):
    n = row.shape[1]
    same = lax.broadcasted_iota(jnp.int32, (n, n), 0) == lax.broadcasted_iota(jnp.int32, (n, n), 1)
    return jnp.broadcast_to(jnp.sum(jnp.where(same, row, 0.0), axis=1, keepdims=True), (n, width))


def depth_matrix(opacity, points):
    absorbers = opacity.shape[0]
    width = 4 * absorbers * LEVELS
    column = lax.broadcasted_iota(jnp.int32, (points, width), 1)
    held = jnp.zeros((points, width), F32)
    for a in range(absorbers):
        value = as_column(opacity[a : a + 1, :] * -LOG2E, width)
        for n, part in enumerate(parts_of(value, 2)):
            for m in range(2):
                held = jnp.where(column // LEVELS == (2 * n + m) * absorbers + a, part.astype(F32), held)
    level = lax.rem(column, LEVELS)
    return jnp.concatenate([jnp.where(level == i, held, 0.0) for i in range(LEVELS)], axis=0).astype(BF)


def sweep(depths, xs, rise, first, frac, kept, below, above, levels, cells):
    points = frac.shape[0]
    halves = below.shape[0]

    def hold(ref, l, value):
        part = jnp.sum(value.reshape(points // 8, 8, cells), axis=0)
        for h in range(halves):
            ref[h, 8 * l : 8 * l + 8, :] = part[:, h * LANES : (h + 1) * LANES]

    lack = frac * first
    through = lack
    for b in range(up_to(levels, LEVELS) // LEVELS):
        trans = jnp.exp2(dot(depths, xs[b], NN))
        for i in range(min(LEVELS, levels - b * LEVELS)):
            l = b * LEVELS + i
            own = trans[i * points : (i + 1) * points]
            kept[l] = own
            through = own * lack
            hold(below, l, through)
            if l + 1 < levels:
                lack = through + frac * rise[l : l + 1, :]
    lack = 0.05 * through
    for l in range(levels - 1, -1, -1):
        through = kept[l] * lack
        hold(above, l, through)
        if l:
            lack = through - frac * rise[l - 1 : l, :]


def taken(below, above, rise, first, frac, enter, h, levels):
    lanes = slice(h * LANES, (h + 1) * LANES)

    def total(ref):
        value = ref[h, pl.ds(0, levels, stride=8), :]
        for g in range(1, 8):
            value = value + ref[h, pl.ds(g, levels, stride=8), :]
        return value

    down, up = total(below), total(above)
    weight = jnp.sum(frac[:, lanes], axis=0, keepdims=True)
    change = weight * rise[0 : levels - 1, lanes]
    enter[0:1, :] = weight * first[:, lanes]
    enter[1:levels, :] = down[: levels - 1] + change
    value = enter[0:levels, :] - down
    enter[0 : levels - 1, :] = up[1:] - change
    enter[levels - 1 : levels, :] = 0.05 * down[levels - 1 :]
    return value + (enter[0:levels, :] - up)


def radiate_kernel(plan, back, devices, levels, cells, arrived, opacity_in, fraction_in, out, opacity, fraction, sems, parts, match, mean, xs, t4, rise, heat, kept, below, above, enter):
    copies = [
        pltpu.make_async_copy(opacity_in, opacity, sems.at[0]),
        pltpu.make_async_copy(fraction_in, fraction, sems.at[1]),
    ]
    for copy in copies:
        copy.start()
    fields = plan.fields
    lane = plan.rest
    slots = devices * CAP
    absorbers, points = opacity.shape
    tails = [arrived[pl.ds(CAP * plan.whole + j, devices, stride=plan.rows), :] for j in range(plan.tail)]
    pick = mask_to(lax.broadcasted_iota(jnp.int32, (8, LANES), 1) == lane - 1)
    for s in range(CAP):
        for k in range(plan.whole + 1):
            if k < plan.whole:
                value = arrived[pl.ds(CAP * k + s, devices, stride=plan.rows), :]
            else:
                value = plan.unpack(tails, s)
            for n, part in enumerate(parts_of(value, 2)):
                first = n * slots + s * devices
                parts[first : first + devices, k * LANES : (k + 1) * LANES] = part
        cell = value[:, lane - 1 : lane].astype(jnp.int32)
        here = mask_to(cell == lax.broadcasted_iota(jnp.int32, (devices, cells), 1))
        for n in range(2):
            match[s * devices : (s + 1) * devices, n * cells : (n + 1) * cells] = here
    cell_row = dot(pick, parts[0:slots, plan.whole * LANES :], NT)[0:1].astype(jnp.int32)
    turned = mask_to(lax.broadcasted_iota(jnp.int32, (cells, slots), 0) == cell_row)
    sums = jnp.transpose(dot(jnp.concatenate([turned, turned], axis=1), parts[...], NN))
    inverse = 1.0 / jnp.maximum(sums[fields - 2 : fields - 1, :], 1.0)
    even = levels // 8 * 8
    block = mean.shape[0]
    spare = (absorbers + 1) * even

    def means(k):
        row = lax.broadcasted_iota(jnp.int32, (block - even, cells), 0)
        mean[0:even, :] = sums[k * even : (k + 1) * even] * inverse
        mean[even:, :] = jnp.where(row == 0, sums[spare + k : spare + k + 1] * inverse, 0.0)
        return mean[...]

    warm = means(0)
    square = warm * warm
    t4[...] = square * square
    rise[0 : levels - 1, :] = t4[1:levels, :] - t4[0 : levels - 1, :]
    for a in range(absorbers):
        for n, part in enumerate(parts_of(means(a + 1), 2)):
            for m in range(2):
                first = ((2 * m + n) * absorbers + a) * LEVELS
                for b in range(block // LEVELS):
                    xs[b, first : first + LEVELS, :] = part[b * LEVELS : (b + 1) * LEVELS]
    for copy in copies:
        copy.wait()
    frac = as_column(fraction[...], cells)
    top = t4[0:1, :]
    sweep(depth_matrix(opacity, points), xs, rise, top, frac, kept, below, above, levels, cells)
    heat[...] = jnp.zeros(heat.shape, BF)
    for h in range(below.shape[0]):
        total = taken(below, above, rise, top, frac, enter, h, levels)
        for n, part in enumerate(parts_of(-total, 2)):
            first = n * cells + h * LANES
            heat[0:levels, first : first + LANES] = part
    acc = dot(match[...], heat[...], NT)
    for s in range(CAP):
        out[pl.ds(s, devices, stride=back.rows), :] = acc[s * devices : (s + 1) * devices, :LANES]
    rests = [acc[s * devices : (s + 1) * devices, LANES:] for s in range(CAP)]
    for j, tile in enumerate(back.pack(rests)):
        out[pl.ds(CAP + j, devices, stride=back.rows), :] = tile


def spread_kernel(back, devices, levels, chunks, returned, ones, slot, out, wide, held, sems):
    rows, columns = held.shape
    pieces = slot.shape[1]
    block = up_to(levels, 16)
    tails = [returned[pl.ds(CAP + j, devices, stride=back.rows), :] for j in range(back.tail)]
    for s in range(CAP):
        own = slice(s * devices, (s + 1) * devices)
        wide[own, :LANES] = returned[pl.ds(s, devices, stride=back.rows), :]
        wide[own, LANES:] = back.unpack(tails, s)
    turned = jnp.transpose(wide[...])[:block]
    both = dot(jnp.concatenate(parts_of(turned, 2), axis=0), slot[...], NN)
    both = jnp.concatenate(parts_of(both[:block] + both[block:], 2), axis=0)
    size = columns // chunks
    copies = []
    for c in range(chunks):
        own = slice(c * size, (c + 1) * size)
        value = dot(both, ones[own, :], NT)
        held[:, own] = value[:rows] + value[block : block + rows]
        copies.append(pltpu.make_async_copy(held.at[:, own], out.at[:, own], sems.at[c]))
        copies[-1].start()
    for copy in copies:
        copy.wait()


VMEM = pl.BlockSpec(memory_space=pltpu.VMEM)
HBM = pl.BlockSpec(memory_space=pl.ANY)


def params(mib):
    return pltpu.CompilerParams(vmem_limit_bytes=mib * MIB)


def in_hbm(value):
    return pltpu.with_memory_space_constraint(value, pltpu.HBM)


def plans(levels, species):
    fields = species * levels + 2
    return Plan(fields, up_to(fields % LANES, 16)), Plan(levels, up_to(levels % LANES, 16))


def gather_call(thermal, gas, weight_row, segment_row, target_row, box_row):
    levels, columns = thermal.shape
    species = gas.shape[1] + 1
    pieces = target_row.shape[1]
    devices = lax.axis_size(AXES)
    plan, _ = plans(levels, species)
    padded = (plan.whole + 1) * LANES
    slots = devices * CAP
    return pl.pallas_call(
        functools.partial(gather_kernel, plan, devices, (2, 3), True),
        out_shape=(
            jax.ShapeDtypeStruct((devices * plan.rows, LANES), F32),
            jax.ShapeDtypeStruct((columns, pieces), BF),
            jax.ShapeDtypeStruct((slots, pieces), BF),
        ),
        in_specs=[HBM] * 6,
        out_specs=(VMEM, VMEM, VMEM),
        scratch_shapes=[
            pltpu.VMEM((species, levels, columns), F32),
            pltpu.SemaphoreType.DMA((species + 4,)),
            pltpu.VMEM((1, columns), F32),
            pltpu.VMEM((1, columns), jnp.int32),
            pltpu.VMEM((1, pieces), jnp.int32),
            pltpu.VMEM((1, pieces), jnp.int32),
            pltpu.VMEM((2 * species * up_to(levels, 16) + 16, columns), BF),
            pltpu.VMEM((padded, pieces), F32),
        ],
        compiler_params=params(34),
        name="gather_pieces",
    )(*map(in_hbm, (thermal, gas, weight_row, segment_row, target_row, box_row)))


def radiate_call(arrived, opacity, fraction, levels, cells):
    absorbers, points = opacity.shape
    species = absorbers + 1
    devices = lax.axis_size(AXES)
    plan, back = plans(levels, species)
    padded = (plan.whole + 1) * LANES
    slots = devices * CAP
    block = up_to(levels, LEVELS)
    return pl.pallas_call(
        functools.partial(radiate_kernel, plan, back, devices, levels, cells),
        out_shape=jax.ShapeDtypeStruct((devices * back.rows, LANES), F32),
        in_specs=[VMEM, HBM, HBM],
        out_specs=VMEM,
        scratch_shapes=[
            pltpu.VMEM((absorbers, points), F32),
            pltpu.VMEM((1, points), F32),
            pltpu.SemaphoreType.DMA((2,)),
            pltpu.VMEM((2 * slots, padded), BF),
            pltpu.VMEM((slots, 2 * cells), BF),
            pltpu.VMEM((block, cells), F32),
            pltpu.VMEM((block // LEVELS, 4 * absorbers * LEVELS, cells), BF),
            pltpu.VMEM((block, cells), F32),
            pltpu.VMEM((block, cells), F32),
            pltpu.VMEM((2 * LANES, 2 * cells), BF),
            pltpu.VMEM((levels, points, cells), F32),
            pltpu.VMEM((cells // LANES, 8 * levels, LANES), F32),
            pltpu.VMEM((cells // LANES, 8 * levels, LANES), F32),
            pltpu.VMEM((block, LANES), F32),
        ],
        compiler_params=params(28),
        name="radiate_cells",
    )(arrived, in_hbm(opacity), in_hbm(fraction))


def spread_call(returned, ones, slot, levels):
    columns, pieces = ones.shape
    slots = slot.shape[0]
    devices = slots // CAP
    _, back = plans(levels, 1)
    chunks = 4
    return pl.pallas_call(
        functools.partial(spread_kernel, back, devices, levels, chunks),
        out_shape=jax.ShapeDtypeStruct((levels, columns), F32),
        in_specs=[VMEM, VMEM, VMEM],
        out_specs=HBM,
        scratch_shapes=[
            pltpu.VMEM((slots, 2 * LANES), F32),
            pltpu.VMEM((levels, columns), F32),
            pltpu.SemaphoreType.DMA((chunks,)),
        ],
        compiler_params=params(16),
        name="spread_heat",
    )(returned, ones, slot)


def exchange(value):
    devices = lax.axis_size(AXES)
    chunks = value.reshape(devices, 1, value.size // devices)
    return lax.all_to_all(chunks, AXES, split_axis=0, concat_axis=0, tiled=True).reshape(value.shape)


def shards(thermal, gas, footprint, segment, holder, box, opacity, fraction):
    levels, columns = thermal.shape
    pieces = box.shape[0]
    outgoing, ones, slot = gather_call(
        thermal,
        gas.transpose(1, 0, 2),
        footprint.reshape(1, columns),
        segment.reshape(1, columns),
        holder.reshape(1, pieces),
        box.reshape(1, pieces),
    )
    arrived = exchange(outgoing)
    heat = radiate_call(arrived, opacity.T, fraction.reshape(1, -1), levels, columns // 8)
    returned = exchange(heat)
    return spread_call(returned, ones, slot, levels)


def solution(mesh):
    placed = (
        P(None, AXES),
        P(None, None, AXES),
        P(AXES),
        P(AXES),
        P(AXES, None),
        P(AXES),
        P(),
        P(),
    )
    return jax.shard_map(shards, mesh=mesh, in_specs=placed, out_specs=P(None, AXES), check_vma=False)
```

```python
import functools

import jax
import jax.numpy as jnp
from jax import lax
from jax.experimental import pallas as pl
from jax.experimental.pallas import tpu as pltpu
from jax.sharding import PartitionSpec as P

AXES = ("dyn", "rad")
CAP = 8
LANES = 128
BF = jnp.bfloat16
F32 = jnp.float32
NT = (((1,), (1,)), ((), ()))
NN = (((1,), (0,)), ((), ()))
MIB = 1024 * 1024
FIRST = 2
BATCHES = {0: 2, 2: 5}
LEVELS = 16
LOG2E = 1.4426950408889634


def up_to(value, step):
    return -(-value // step) * step


def parts_of(value, count):
    out = []
    for _ in range(count - 1):
        part = value.astype(BF)
        out.append(part)
        value = value - part.astype(F32)
    out.append(value.astype(BF))
    return out


def mask_to(mask):
    return jnp.where(mask, 1.0, 0.0).astype(BF)


def dot(a, b, dims):
    return lax.dot_general(a, b, dims, preferred_element_type=F32)


def slots_of(target, devices):
    pieces = target.shape[1]
    column = jnp.transpose(jnp.broadcast_to(target, (LANES, pieces)))
    ranks = []
    for j in range(pieces // LANES):
        part = target[:, j * LANES : (j + 1) * LANES]
        before = lax.broadcasted_iota(jnp.int32, (pieces, LANES), 0)
        me = lax.broadcasted_iota(jnp.int32, (pieces, LANES), 1) + j * LANES
        hit = (column == part) & (before < me)
        ranks.append(jnp.sum(jnp.where(hit, 1, 0), axis=0, keepdims=True))
    return jnp.concatenate(ranks, axis=1)


def slot_rows(target, rank, devices, store):
    pieces = target.shape[1]
    owner = lax.broadcasted_iota(jnp.int32, (devices, pieces), 0) == target
    for s in range(CAP):
        store(s, mask_to(owner & (rank == s)))


class Plan:
    def __init__(self, fields, width):
        self.fields = fields
        self.whole = fields // LANES
        self.rest = fields - self.whole * LANES
        self.width = width
        self.tail = up_to(CAP * width, LANES) // LANES
        self.rows = CAP * self.whole + self.tail

    def spans(self, s):
        start = s * self.width
        first, shift = start // LANES, start % LANES
        yield first, shift, None if shift + self.width <= LANES else "low"
        if shift + self.width > LANES:
            yield first + 1, shift, "high"

    def pack(self, rests):
        lane = lax.broadcasted_iota(jnp.int32, rests[0].shape, 1)
        tiles = [None] * self.tail
        for s, rest in enumerate(rests):
            for tile, shift, side in self.spans(s):
                part = pltpu.roll(rest, shift, 1) if shift else rest
                if side == "low":
                    part = jnp.where(lane >= shift, part, 0.0)
                if side == "high":
                    part = jnp.where(lane < shift, part, 0.0)
                tiles[tile] = part if tiles[tile] is None else tiles[tile] + part
        return tiles

    def unpack(self, tiles, s):
        spans = list(self.spans(s))
        value, shift = tiles[spans[0][0]], spans[0][1]
        if len(spans) == 2:
            lane = lax.broadcasted_iota(jnp.int32, value.shape, 1)
            value = jnp.where(lane >= shift, value, tiles[spans[1][0]])
        return pltpu.roll(value, LANES - shift, 1) if shift else value


def gather_kernel(plan, devices, groups, late, thermal, gas, weight_in, segment_in, target_in, box_in, out, ones, slot, buf, sems, weight, segment, target, box, left, comp):
    species, levels, columns = buf.shape
    pieces = target.shape[1]
    block = up_to(levels, 16)
    small = [(segment_in, segment), (weight_in, weight), (target_in, target), (box_in, box)]
    rows = [pltpu.make_async_copy(a, b, sems.at[species + n]) for n, (a, b) in enumerate(small)]
    for copy in rows:
        copy.start()
    copies = [pltpu.make_async_copy(thermal, buf.at[0], sems.at[0])]
    copies += [pltpu.make_async_copy(gas.at[:, k, :], buf.at[k + 1], sems.at[k + 1]) for k in range(species - 1)]
    for copy in copies[:FIRST]:
        copy.start()
    for copy in rows:
        copy.wait()
    for copy in copies[FIRST:]:
        copy.start()
    down = jnp.transpose(jnp.broadcast_to(segment[...], (LANES, columns)))
    for k in range(pieces // LANES):
        lane = lax.broadcasted_iota(jnp.int32, (columns, LANES), 1) + k * LANES
        ones[:, k * LANES : (k + 1) * LANES] = mask_to(down == lane)
    w = weight[...]
    end = 2 * species * block
    pair = parts_of(jnp.broadcast_to(w, (8, columns)), 2)
    left[end:, :] = jnp.concatenate([part.astype(F32) for part in pair], axis=0).astype(BF)

    def place():
        owner = target[...]
        rank = slots_of(owner, devices)

        def store(s, value):
            slot[s * devices : (s + 1) * devices, :] = value

        slot_rows(owner, rank, devices, store)

    def load(k):
        if k in BATCHES:
            for copy in copies[k : BATCHES[k]]:
                copy.wait()
        for n, part in enumerate(parts_of(buf[k] * w, 2)):
            left[(2 * k + n) * block : (2 * k + n) * block + levels, :] = part

    even = levels // 8 * 8
    spare = species * even

    def keep(k, sums, a):
        pair = sums[a : a + levels] + sums[a + block : a + block + levels]
        comp[k * even : (k + 1) * even, :] = pair[:even]
        return pair[even:]

    wide = 2 * LANES

    def emit(k):
        pair = parts_of(comp[k * wide : (k + 1) * wide, :], 2)
        acc = dot(slot[...], pair[0], NT) + dot(slot[...], pair[1], NT)
        for h in range(2):
            tile = 2 * k + h
            values = [acc[s * devices : (s + 1) * devices, h * LANES : (h + 1) * LANES] for s in range(CAP)]
            if tile < plan.whole:
                for s in range(CAP):
                    out[pl.ds(CAP * tile + s, devices, stride=plan.rows), :] = values[s]
            else:
                for j, value in enumerate(plan.pack(values)):
                    out[pl.ds(CAP * tile + j, devices, stride=plan.rows), :] = value

    emitted = 0
    ends = []
    bounds = [sum(groups[:n]) for n in range(len(groups) + 1)]
    for begin, stop in zip(bounds, bounds[1:]):
        last = stop == species
        for k in range(begin, stop):
            load(k)
        if begin == 0:
            place()
        sums = dot(left[2 * begin * block : end + 16 if last else 2 * stop * block, :], ones[...], NN)
        for k in range(begin, stop):
            a = 2 * (k - begin) * block
            ends.append(keep(k, sums, a))
        if last:
            a = 2 * (stop - begin) * block
            ends.append(sums[a : a + 1] + sums[a + 8 : a + 9])
            ends.append(box[...].astype(F32))
            row = lax.broadcasted_iota(jnp.int32, (comp.shape[0] - spare, pieces), 0)
            rest = jnp.zeros(row.shape, F32)
            for n, value in enumerate(ends):
                rest = jnp.where(row == n, value, rest)
            comp[spare:, :] = rest
        ready = comp.shape[0] if last or late else stop * even
        while (emitted + 1) * wide <= ready and (last or not late):
            emit(emitted)
            emitted += 1


def as_column(row, width):
    n = row.shape[1]
    same = lax.broadcasted_iota(jnp.int32, (n, n), 0) == lax.broadcasted_iota(jnp.int32, (n, n), 1)
    return jnp.broadcast_to(jnp.sum(jnp.where(same, row, 0.0), axis=1, keepdims=True), (n, width))


def depth_matrix(opacity, points):
    absorbers = opacity.shape[0]
    width = 4 * absorbers * LEVELS
    column = lax.broadcasted_iota(jnp.int32, (points, width), 1)
    held = jnp.zeros((points, width), F32)
    for a in range(absorbers):
        value = as_column(opacity[a : a + 1, :] * -LOG2E, width)
        for n, part in enumerate(parts_of(value, 2)):
            for m in range(2):
                held = jnp.where(column // LEVELS == (2 * n + m) * absorbers + a, part.astype(F32), held)
    level = lax.rem(column, LEVELS)
    return jnp.concatenate([jnp.where(level == i, held, 0.0) for i in range(LEVELS)], axis=0).astype(BF)


def sweep(depths, xs, rise, first, frac, kept, below, above, levels, cells):
    points = frac.shape[0]
    halves = below.shape[0]

    def hold(ref, l, value):
        part = jnp.sum(value.reshape(points // 8, 8, cells), axis=0)
        for h in range(halves):
            ref[h, 8 * l : 8 * l + 8, :] = part[:, h * LANES : (h + 1) * LANES]

    lack = frac * first
    through = lack
    for b in range(up_to(levels, LEVELS) // LEVELS):
        trans = jnp.exp2(dot(depths, xs[b], NN))
        for i in range(min(LEVELS, levels - b * LEVELS)):
            l = b * LEVELS + i
            own = trans[i * points : (i + 1) * points]
            kept[l] = own
            through = own * lack
            hold(below, l, through)
            if l + 1 < levels:
                lack = through + frac * rise[l : l + 1, :]
    lack = 0.05 * through
    for l in range(levels - 1, -1, -1):
        through = kept[l] * lack
        hold(above, l, through)
        if l:
            lack = through - frac * rise[l - 1 : l, :]


def taken(below, above, rise, first, frac, enter, h, levels):
    lanes = slice(h * LANES, (h + 1) * LANES)

    def total(ref):
        value = ref[h, pl.ds(0, levels, stride=8), :]
        for g in range(1, 8):
            value = value + ref[h, pl.ds(g, levels, stride=8), :]
        return value

    down, up = total(below), total(above)
    weight = jnp.sum(frac[:, lanes], axis=0, keepdims=True)
    change = weight * rise[0 : levels - 1, lanes]
    enter[0:1, :] = weight * first[:, lanes]
    enter[1:levels, :] = down[: levels - 1] + change
    value = enter[0:levels, :] - down
    enter[0 : levels - 1, :] = up[1:] - change
    enter[levels - 1 : levels, :] = 0.05 * down[levels - 1 :]
    return value + (enter[0:levels, :] - up)


def radiate_kernel(plan, back, devices, levels, cells, arrived, opacity_in, fraction_in, out, opacity, fraction, sems, parts, match, mean, xs, t4, rise, heat, kept, below, above, enter):
    copies = [
        pltpu.make_async_copy(opacity_in, opacity, sems.at[0]),
        pltpu.make_async_copy(fraction_in, fraction, sems.at[1]),
    ]
    for copy in copies:
        copy.start()
    fields = plan.fields
    lane = plan.rest
    slots = devices * CAP
    absorbers, points = opacity.shape
    tails = [arrived[pl.ds(CAP * plan.whole + j, devices, stride=plan.rows), :] for j in range(plan.tail)]
    pick = mask_to(lax.broadcasted_iota(jnp.int32, (8, LANES), 1) == lane - 1)
    for s in range(CAP):
        for k in range(plan.whole + 1):
            if k < plan.whole:
                value = arrived[pl.ds(CAP * k + s, devices, stride=plan.rows), :]
            else:
                value = plan.unpack(tails, s)
            for n, part in enumerate(parts_of(value, 2)):
                first = n * slots + s * devices
                parts[first : first + devices, k * LANES : (k + 1) * LANES] = part
        cell = value[:, lane - 1 : lane].astype(jnp.int32)
        here = mask_to(cell == lax.broadcasted_iota(jnp.int32, (devices, cells), 1))
        match[s * devices : (s + 1) * devices, :] = here
    cell_row = dot(pick, parts[0:slots, plan.whole * LANES :], NT)[0:1].astype(jnp.int32)
    turned = mask_to(lax.broadcasted_iota(jnp.int32, (cells, slots), 0) == cell_row)
    sums = jnp.transpose(dot(jnp.concatenate([turned, turned], axis=1), parts[...], NN))
    inverse = 1.0 / jnp.maximum(sums[fields - 2 : fields - 1, :], 1.0)
    even = levels // 8 * 8
    block = mean.shape[0]
    spare = (absorbers + 1) * even

    def means(k):
        row = lax.broadcasted_iota(jnp.int32, (block - even, cells), 0)
        mean[0:even, :] = sums[k * even : (k + 1) * even] * inverse
        mean[even:, :] = jnp.where(row == 0, sums[spare + k : spare + k + 1] * inverse, 0.0)
        return mean[...]

    warm = means(0)
    square = warm * warm
    t4[...] = square * square
    rise[0 : levels - 1, :] = t4[1:levels, :] - t4[0 : levels - 1, :]
    for a in range(absorbers):
        for n, part in enumerate(parts_of(means(a + 1), 2)):
            for m in range(2):
                first = ((2 * m + n) * absorbers + a) * LEVELS
                for b in range(block // LEVELS):
                    xs[b, first : first + LEVELS, :] = part[b * LEVELS : (b + 1) * LEVELS]
    for copy in copies:
        copy.wait()
    frac = as_column(fraction[...], cells)
    top = t4[0:1, :]
    sweep(depth_matrix(opacity, points), xs, rise, top, frac, kept, below, above, levels, cells)
    heat[...] = jnp.zeros(heat.shape, BF)
    for h in range(below.shape[0]):
        total = taken(below, above, rise, top, frac, enter, h, levels)
        for n, part in enumerate(parts_of(-total, 2)):
            first = n * cells + h * LANES
            heat[0:levels, first : first + LANES] = part
    acc = dot(match[...], heat[:, :cells], NT) + dot(match[...], heat[:, cells:], NT)
    for s in range(CAP):
        out[pl.ds(s, devices, stride=back.rows), :] = acc[s * devices : (s + 1) * devices, :LANES]
    rests = [acc[s * devices : (s + 1) * devices, LANES:] for s in range(CAP)]
    for j, tile in enumerate(back.pack(rests)):
        out[pl.ds(CAP + j, devices, stride=back.rows), :] = tile


def spread_kernel(back, devices, levels, chunks, returned, ones, slot, out, wide, held, sems):
    rows, columns = held.shape
    pieces = slot.shape[1]
    block = up_to(levels, 16)
    tails = [returned[pl.ds(CAP + j, devices, stride=back.rows), :] for j in range(back.tail)]
    for s in range(CAP):
        own = slice(s * devices, (s + 1) * devices)
        wide[own, :LANES] = returned[pl.ds(s, devices, stride=back.rows), :]
        wide[own, LANES:] = back.unpack(tails, s)
    turned = jnp.transpose(wide[...])[:block]
    both = dot(jnp.concatenate(parts_of(turned, 2), axis=0), slot[...], NN)
    both = jnp.concatenate(parts_of(both[:block] + both[block:], 2), axis=0)
    size = columns // chunks
    copies = []
    for c in range(chunks):
        own = slice(c * size, (c + 1) * size)
        value = dot(both, ones[own, :], NT)
        held[:, own] = value[:rows] + value[block : block + rows]
        copies.append(pltpu.make_async_copy(held.at[:, own], out.at[:, own], sems.at[c]))
        copies[-1].start()
    for copy in copies:
        copy.wait()


VMEM = pl.BlockSpec(memory_space=pltpu.VMEM)
HBM = pl.BlockSpec(memory_space=pl.ANY)


def params(mib):
    return pltpu.CompilerParams(vmem_limit_bytes=mib * MIB)


def in_hbm(value):
    return pltpu.with_memory_space_constraint(value, pltpu.HBM)


def plans(levels, species):
    fields = species * levels + 2
    return Plan(fields, up_to(fields % LANES, 16)), Plan(levels, up_to(levels % LANES, 16))


def gather_call(thermal, gas, weight_row, segment_row, target_row, box_row):
    levels, columns = thermal.shape
    species = gas.shape[1] + 1
    pieces = target_row.shape[1]
    devices = lax.axis_size(AXES)
    plan, _ = plans(levels, species)
    padded = (plan.whole + 1) * LANES
    slots = devices * CAP
    return pl.pallas_call(
        functools.partial(gather_kernel, plan, devices, (2, 3), True),
        out_shape=(
            jax.ShapeDtypeStruct((devices * plan.rows, LANES), F32),
            jax.ShapeDtypeStruct((columns, pieces), BF),
            jax.ShapeDtypeStruct((slots, pieces), BF),
        ),
        in_specs=[HBM] * 6,
        out_specs=(VMEM, VMEM, VMEM),
        scratch_shapes=[
            pltpu.VMEM((species, levels, columns), F32),
            pltpu.SemaphoreType.DMA((species + 4,)),
            pltpu.VMEM((1, columns), F32),
            pltpu.VMEM((1, columns), jnp.int32),
            pltpu.VMEM((1, pieces), jnp.int32),
            pltpu.VMEM((1, pieces), jnp.int32),
            pltpu.VMEM((2 * species * up_to(levels, 16) + 16, columns), BF),
            pltpu.VMEM((padded, pieces), F32),
        ],
        compiler_params=params(34),
        name="gather_pieces",
    )(*map(in_hbm, (thermal, gas, weight_row, segment_row, target_row, box_row)))


def radiate_call(arrived, opacity, fraction, levels, cells):
    absorbers, points = opacity.shape
    species = absorbers + 1
    devices = lax.axis_size(AXES)
    plan, back = plans(levels, species)
    padded = (plan.whole + 1) * LANES
    slots = devices * CAP
    block = up_to(levels, LEVELS)
    return pl.pallas_call(
        functools.partial(radiate_kernel, plan, back, devices, levels, cells),
        out_shape=jax.ShapeDtypeStruct((devices * back.rows, LANES), F32),
        in_specs=[VMEM, HBM, HBM],
        out_specs=VMEM,
        scratch_shapes=[
            pltpu.VMEM((absorbers, points), F32),
            pltpu.VMEM((1, points), F32),
            pltpu.SemaphoreType.DMA((2,)),
            pltpu.VMEM((2 * slots, padded), BF),
            pltpu.VMEM((slots, cells), BF),
            pltpu.VMEM((block, cells), F32),
            pltpu.VMEM((block // LEVELS, 4 * absorbers * LEVELS, cells), BF),
            pltpu.VMEM((block, cells), F32),
            pltpu.VMEM((block, cells), F32),
            pltpu.VMEM((2 * LANES, 2 * cells), BF),
            pltpu.VMEM((levels, points, cells), F32),
            pltpu.VMEM((cells // LANES, 8 * levels, LANES), F32),
            pltpu.VMEM((cells // LANES, 8 * levels, LANES), F32),
            pltpu.VMEM((block, LANES), F32),
        ],
        compiler_params=params(28),
        name="radiate_cells",
    )(arrived, in_hbm(opacity), in_hbm(fraction))


def spread_call(returned, ones, slot, levels):
    columns, pieces = ones.shape
    slots = slot.shape[0]
    devices = slots // CAP
    _, back = plans(levels, 1)
    chunks = 4
    return pl.pallas_call(
        functools.partial(spread_kernel, back, devices, levels, chunks),
        out_shape=jax.ShapeDtypeStruct((levels, columns), F32),
        in_specs=[VMEM, VMEM, VMEM],
        out_specs=HBM,
        scratch_shapes=[
            pltpu.VMEM((slots, 2 * LANES), F32),
            pltpu.VMEM((levels, columns), F32),
            pltpu.SemaphoreType.DMA((chunks,)),
        ],
        compiler_params=params(16),
        name="spread_heat",
    )(returned, ones, slot)


def exchange(value):
    devices = lax.axis_size(AXES)
    chunks = value.reshape(devices, 1, value.size // devices)
    return lax.all_to_all(chunks, AXES, split_axis=0, concat_axis=0, tiled=True).reshape(value.shape)


def shards(thermal, gas, footprint, segment, holder, box, opacity, fraction):
    levels, columns = thermal.shape
    pieces = box.shape[0]
    outgoing, ones, slot = gather_call(
        thermal,
        gas.transpose(1, 0, 2),
        footprint.reshape(1, columns),
        segment.reshape(1, columns),
        holder.reshape(1, pieces),
        box.reshape(1, pieces),
    )
    arrived = exchange(outgoing)
    heat = radiate_call(arrived, opacity.T, fraction.reshape(1, -1), levels, columns // 8)
    returned = exchange(heat)
    return spread_call(returned, ones, slot, levels)


def solution(mesh):
    placed = (
        P(None, AXES),
        P(None, None, AXES),
        P(AXES),
        P(AXES),
        P(AXES, None),
        P(AXES),
        P(),
        P(),
    )
    return jax.shard_map(shards, mesh=mesh, in_specs=placed, out_specs=P(None, AXES), check_vma=False)
```
